128 devices in a mesh: row: 16 (over z_lo, y, core), col: 8 (over x, z_hi).
Axes of the slice: x: 4, y: 4, z: 4 (z_hi: 2, z_lo: 2; z = z_hi * 2 + z_lo), core: 2. Of those that a mesh axis runs over, the one named last changes fastest.
Arguments:
- hamiltonian: bfloat16 [8192, 8192], P('row', 'col'), may hold values from -1 to 1, as said below
- block_cols: int32 [128, 26], P('row'), may hold values from 0 to 127, as said below
- start_vectors: bfloat16 [8192, 2048], P('col'), may hold values from -6 to 6
Outputs:
- filtered: bfloat16 [8192, 2048], P('col')
- correlation: float32 [2048, 2048], P('row', 'col')
- projected: float32 [2048, 2048], P('row', 'col')
The draws below stay inside these ranges and needn't reach their ends.
Inputs may be any that keep to these rules, and one draw needn't show every extreme that they name: `block_cols`: along the last dimension, 26 distinct block columns in increasing order; block row i lists itself, and lists j exactly when block row j lists i. `hamiltonian`: Symmetric.
All inputs are finite; a program needn't handle non-finite values.
Results may differ from the reference program's by a relative error of at most 0.02.
Values may be sent and summed in bfloat16 or wider, within the bound.
A program may use at most 128 MiB of HBM per device.

```python
import math
import jax
import jax.numpy as jnp
from jax import lax

BLK = 64
M = 2048
CBLK = 16
HALF_NB = 12
K_NB = 26
NBLK = 128
N = 8192


def tile_pattern(key):
    offset_key, order_key = jax.random.split(key)
    near_offsets = jax.random.permutation(offset_key, CBLK)[:HALF_NB].astype(jnp.int32) + 1
    far_offset = jnp.array([NBLK // 2], dtype=jnp.int32)
    choices_made = jnp.concatenate((near_offsets, far_offset))
    indices = jnp.arange(NBLK, dtype=jnp.int32)
    distance = (indices[None, :] - indices[:, None]) % NBLK
    distance = jnp.minimum(distance, NBLK - distance)
    base = (distance == 0) | jnp.any(distance[:, :, None] == choices_made[None, None, :], axis=2)
    relabel = jax.random.permutation(order_key, NBLK).astype(jnp.int32)
    return base[relabel][:, relabel]


def draw_hamiltonian(key, part):
    pattern = tile_pattern(key)
    key = jax.random.fold_in(key, 7)
    entries = jax.random.normal(key, (N, N), jnp.float32)
    spread = 0.5 / math.sqrt(K_NB * BLK)
    symmetric = (entries + entries.T) * (spread / math.sqrt(2.0))
    full_mask = jnp.repeat(jnp.repeat(pattern, BLK, axis=0), BLK, axis=1)
    return jnp.where(full_mask, symmetric, 0.0).astype(jnp.bfloat16)


def draw_block_cols(key, part):
    pattern = tile_pattern(key)
    positions = jnp.arange(NBLK, dtype=jnp.int32)
    scores = jnp.where(pattern, positions[None, :], NBLK + positions[None, :])
    return jnp.sort(scores, axis=-1)[:, :K_NB].astype(jnp.int32)


def levels(own_key, shape, pieces, low, high):
    def one(dim, parts):
        heights = jax.random.uniform(jax.random.fold_in(jax.random.fold_in(own_key, 6), dim), (parts,), jnp.float32, low / len(pieces), high / len(pieces))
        return jnp.repeat(jnp.exp(heights), shape[dim] // parts).reshape((-1,) + (1,) * (len(shape) - dim - 1))

    level = one(*pieces[0])
    for cut in pieces[1:]:
        level = level * one(*cut)
    return level


def centred(rng, extent, width, limit, shards=(), kind=jnp.bfloat16):
    drawn = width * jax.random.normal(rng, extent, jnp.float32)
    if shards:
        drawn = drawn * levels(rng, extent, shards, -0.22, 0.18)
    return jnp.clip(drawn, -limit, limit).astype(kind)


def setup_inputs(seed: int = 0) -> dict:
    keys = jax.random.split(jax.random.key(seed), 4)
    hamiltonian = draw_hamiltonian(jax.random.fold_in(keys[3], 71), 0)
    block_cols = draw_block_cols(jax.random.fold_in(keys[3], 71), 0)
    start_vectors = centred(keys[2], (N, M), 1.0, 6.0, ((0, 8),))
    return {"hamiltonian": hamiltonian, "block_cols": block_cols, "start_vectors": start_vectors}


center_point = 0.2
half_width = 0.8


def listed_mask(block_cols):
    block_count = block_cols.shape[0]
    matches = block_cols[:, :, None] == jnp.arange(block_count, dtype=jnp.int32)[None, None, :]
    return jnp.any(matches, axis=1)


def reference(hamiltonian, block_cols, start_vectors):
    block_mask = listed_mask(block_cols)
    full_mask = jnp.repeat(jnp.repeat(block_mask, BLK, axis=0), BLK, axis=1)
    masked = jnp.where(full_mask, hamiltonian, jnp.zeros_like(hamiltonian)).astype(jnp.float32)
    start_wide = start_vectors.astype(jnp.float32)
    highest = lax.Precision.HIGHEST
    section_one = (jnp.dot(masked, start_wide, precision=highest) - center_point * start_wide) / half_width
    section_one = section_one.astype(jnp.bfloat16).astype(jnp.float32)
    filtered = (2.0 / half_width) * (jnp.dot(masked.T, section_one, precision=highest) - center_point * section_one) - start_wide
    filtered = filtered.astype(jnp.bfloat16)
    filtered_wide = filtered.astype(jnp.float32)
    image = jnp.dot(masked, filtered_wide, precision=highest).astype(jnp.bfloat16).astype(jnp.float32)
    correlation = jnp.dot(filtered_wide.T, filtered_wide, precision=highest) / N
    projected = jnp.dot(filtered_wide.T, image, precision=highest) / N
    return (filtered, correlation, projected)
```

```python
import functools

import jax
import jax.numpy as jnp
from jax import lax
from jax.experimental import pallas as pl
from jax.experimental.pallas import tpu as pltpu
from jax.sharding import PartitionSpec as P

BLK = 64
K_NB = 26
DEPTH = K_NB * BLK
MESH = pl.DeviceIdType.MESH
center_point = 0.2
half_width = 0.8


class Gather:
    def __init__(self, slot, p, w, pair, right, left, send_sem, recv_sem, pending):
        self.slot, self.p, self.w = slot, p, w
        self.pair, self.right, self.left = pair, right, left
        self.send_sem, self.recv_sem, self.pending = send_sem, recv_sem, pending

    def at(self, dp, dw):
        return lax.rem(self.p + dp + 4, 4), (self.w + dw) % 2

    def sent(self, i):
        return self.at(*((0, 0), (0, 0), (0, 0), (0, 1), (0, 1), (-1, 0), (1, 1))[i])

    def received(self, i):
        return self.at(*((0, 1), (-1, 0), (1, 0), (-1, 1), (1, 1), (2, 0), (2, 1))[i])

    def send(self, i, chunk=0, src=None):
        dst = self.slot(*self.sent(i), chunk)
        to = self.pair if i == 0 else (self.right if i % 2 else self.left)
        copy = pltpu.make_async_remote_copy(
            src_ref=dst if src is None else src,
            dst_ref=dst,
            send_sem=self.send_sem.at[i, chunk],
            recv_sem=self.recv_sem.at[i, chunk],
            device_id=to,
            device_id_type=MESH,
        )
        copy.start()
        self.pending.append(copy)

    def wait(self, i, chunk=0):
        ref = self.slot(*self.received(i), chunk)
        pltpu.make_async_remote_copy(
            src_ref=ref,
            dst_ref=ref,
            send_sem=self.send_sem.at[i, chunk],
            recv_sem=self.recv_sem.at[i, chunk],
            device_id=self.pair,
            device_id_type=MESH,
        ).wait_recv()


def kernel(
    h_ref, lists_ref, x_ref, f_ref, corr_ref, proj_ref,
    panels, lists, sib_list, index, halves, sib_half, packed, xs, ss, fs, rows, image, stack,
    turned, part, parts,
    own_sem, panel_sems, list_sems, sib_list_sem, index_sem, half_sem, h_sems, h_sib_sems,
    x_sems, s_sems, f_sems, r_sems, r_sib_sems, part_sems, out_sem,
):
    r = lax.axis_index("row")
    c = lax.axis_index("col")
    k = lax.rem(r, 2)
    chip = r // 2
    y = lax.rem(chip, 4)
    zl = r // 8
    x = c // 2
    zh = lax.rem(c, 2)
    sibling = (r + 1 - 2 * k, c)
    pending = []

    def ring(v, d):
        return lax.rem(v + d + 4, 4)

    def row_device(z, yy):
        return (z * 8 + yy * 2 + k, c)

    def col_device(xx, z):
        return (r, xx * 2 + z)

    def remote(src, dst, sems, i, to, start=True):
        copy = pltpu.make_async_remote_copy(
            src_ref=src, dst_ref=dst, send_sem=sems.at[0, i], recv_sem=sems.at[1, i],
            device_id=to, device_id_type=MESH,
        )
        if start:
            copy.start()
            pending.append(copy)
        return copy

    row_peers = [((zl + dz) % 2, ring(y, dy)) for dz in (1, 0) for dy in (0, 1, 3, 2) if dz or dy]
    col_peers = [(ring(x, dx), (zh + dw) % 2) for dw in (1, 0) for dx in (2, 1, 3, 0) if dw or dx]

    own_panel = pltpu.make_async_copy(
        h_ref.at[:, :, pl.ds(pl.multiple_of((2 * y + zl) * 128, 128), 128)],
        panels.at[pl.ds(chip * 8, 8)], own_sem.at[0],
    )
    own_panel.start()
    x_src = x_ref.at[:, :, pl.ds(pl.multiple_of(r * 128, 128), 128)]
    own_x = pltpu.make_async_copy(x_src, xs.at[pl.ds(c * 16, 16)], own_sem.at[1])
    own_x.start()
    lists[chip] = jnp.zeros((8, 128), jnp.int32)
    lists[chip, :, :K_NB] = lists_ref[...]
    panels[64] = jnp.zeros((BLK, 128), jnp.bfloat16)

    barrier = pltpu.get_barrier_semaphore()
    for z, yy in row_peers:
        pl.semaphore_signal(barrier, inc=1, device_id=row_device(z, yy), device_id_type=MESH)
    for xx, z in col_peers:
        pl.semaphore_signal(barrier, inc=1, device_id=col_device(xx, z), device_id_type=MESH)
    pl.semaphore_signal(barrier, inc=1, device_id=sibling, device_id_type=MESH)
    pl.semaphore_wait(barrier, 15)

    list_copies, panel_copies = [], []
    for i, (z, yy) in enumerate(row_peers):
        list_copies.append(remote(lists.at[chip], lists.at[chip], list_sems, i, row_device(z, yy)))
    for i, (z, yy) in enumerate(row_peers):
        src = h_ref.at[:, :, pl.ds(pl.multiple_of((2 * yy + z) * 128, 128), 128)]
        panel_copies.append(remote(src, panels.at[pl.ds(chip * 8, 8)], panel_sems, i, row_device(z, yy)))

    def col_gather(buffer, sems, size, order):
        def slot(p, w, t):
            return buffer.at[pl.ds((p * 2 + w) * 16 + order[t] * size, size)]

        return Gather(slot, x, zh, col_device(x, 1 - zh), col_device(ring(x, 1), zh), col_device(ring(x, -1), zh),
                      sems.at[0], sems.at[1], pending)

    gx = col_gather(xs, x_sems, 16, (0,))
    for i in range(3):
        gx.send(i, 0, x_src)

    for copy in list_copies:
        copy.wait_recv()
    sib_lists = remote(lists.at[c], sib_list, sib_list_sem, 0, sibling)
    mine = pltpu.make_async_copy(lists.at[c], index.at[pl.ds(k * 8, 8)], index_sem.at[0])
    mine.start()
    sib_lists.wait_recv()
    theirs = pltpu.make_async_copy(sib_list, index.at[pl.ds((1 - k) * 8, 8)], index_sem.at[1])
    theirs.start()
    mine.wait()
    theirs.wait()

    own_x.wait()
    gx.wait(0)
    gx.send(3)
    gx.send(4)
    gx.wait(1)
    gx.send(5)

    own_panel.wait()
    for copy in panel_copies:
        copy.wait_recv()
    pair_column = 4 * y + 2 * zl
    lane = lax.broadcasted_iota(jnp.int32, (BLK, 128), 1)
    line = lax.broadcasted_iota(jnp.int32, (BLK, 128), 0)
    for side in range(2):
        for s in range(K_NB):
            i = index[pair_column + side, s]
            local = jnp.where(lax.rem(i // 8, 2) == k, 8 * (i // 16) + lax.rem(i, 8), 64)
            stack[s * BLK:(s + 1) * BLK, :] = panels[local]
        pick = (lane == line + BLK * side).astype(jnp.bfloat16)
        halves[side] = lax.dot_general(
            pick, stack[...], (((1,), (1,)), ((), ())), preferred_element_type=jnp.float32
        ).astype(jnp.bfloat16)
    swap = remote(halves.at[1 - k], sib_half, half_sem, 0, sibling)
    swap.wait_recv()
    packed[pair_column + k] = halves[k] + sib_half[...]

    def h_slot(p, w, t):
        return packed.at[p * 4 + w * 2 + k]

    def row_gather(slot, sems):
        return Gather(slot, y, zl, row_device(1 - zl, y), row_device(zl, ring(y, 1)), row_device(zl, ring(y, -1)),
                      sems.at[0], sems.at[1], pending)

    gh = row_gather(h_slot, h_sems)
    h_sib = {}

    def pass_h(i):
        slot = h_slot(y, zl, 0) if i == 0 else h_slot(*gh.received(i - 1), 0)
        h_sib[i] = remote(slot, slot, h_sib_sems, i, sibling)

    for i in range(3):
        gh.send(i)
    pass_h(0)

    gx.wait(2)
    gx.wait(3)
    gx.wait(4)
    gx.send(6)

    def product(source, column):
        for s in range(K_NB):
            stack[s * BLK:(s + 1) * BLK, :] = source[index[column, s]]
        return jnp.dot(packed[column], stack[...], preferred_element_type=jnp.float32)

    order = (y, ring(y, -1), ring(y, 1), ring(y, 2))
    gs = col_gather(ss, s_sems, 4, order)

    def first_degree(t):
        @pl.loop(0, 4)
        def _(j):
            column = order[t] * 4 + j
            at = c * 16 + column
            total = product(xs, column) - center_point * xs[at].astype(jnp.float32)
            ss[at] = (total / half_width).astype(jnp.bfloat16)

        for i in range(3):
            gs.send(i, t)

    def early(g, t):
        g.wait(0, t)
        g.send(3, t)
        g.send(4, t)
        g.wait(1, t)
        g.send(5, t)

    def late(g, t):
        g.wait(4, t)
        g.send(6, t)

    def rest(g, t):
        for i in (2, 3, 5, 6):
            g.wait(i, t)

    gh.wait(0)
    gh.send(3)
    gh.send(4)
    pass_h(1)
    gx.wait(5)
    gx.wait(6)
    h_sib[0].wait_recv()
    h_sib[1].wait_recv()
    first_degree(0)
    gh.wait(1)
    gh.send(5)
    pass_h(2)
    gh.wait(2)
    pass_h(3)
    gh.wait(4)
    gh.send(6)
    pass_h(5)
    gh.wait(3)
    pass_h(4)
    early(gs, 0)
    h_sib[2].wait_recv()
    h_sib[4].wait_recv()
    first_degree(1)
    h_sib[3].wait_recv()
    h_sib[5].wait_recv()
    first_degree(2)
    late(gs, 0)
    early(gs, 1)
    gh.wait(5)
    pass_h(6)
    gh.wait(6)
    pass_h(7)
    early(gs, 2)
    h_sib[6].wait_recv()
    h_sib[7].wait_recv()
    first_degree(3)
    late(gs, 1)
    late(gs, 2)
    early(gs, 3)
    late(gs, 3)
    for t in range(4):
        rest(gs, t)

    gf = col_gather(fs, f_sems, 4, (0, 1, 2, 3))

    def r_slot(parity):
        def slot(p, w, t):
            return rows.at[w * 8 + p * 2 + parity, pl.ds(4 * t, 4)]

        return slot

    gr = row_gather(r_slot(k), r_sems)
    r_sib = {}

    def pass_r(i, t):
        place = (y, zl) if i == 0 else gr.received(i - 1)
        slot = r_slot(k)(*place, t)
        r_sib[i, t] = remote(slot, slot, r_sib_sems, i * 4 + t, sibling)

    for t in range(4):
        @pl.loop(0, 4)
        def _(j):
            column = t * 4 + j
            at = c * 16 + column
            total = product(ss, column) - center_point * ss[at].astype(jnp.float32)
            out = ((2.0 / half_width) * total - xs[at].astype(jnp.float32)).astype(jnp.bfloat16)
            fs[at] = out
            rows[r, column] = out

        for i in range(3):
            gf.send(i, t)
            gr.send(i, t)
        pass_r(0, t)

    for t in range(4):
        early(gf, t)
        early(gr, t)
        pass_r(1, t)
        pass_r(2, t)
        gr.wait(2, t)
        pass_r(3, t)
    for t in range(4):
        late(gf, t)
        late(gr, t)
        pass_r(5, t)
        gr.wait(3, t)
        pass_r(4, t)
    outs = []

    def write_out(group, i):
        copy = pltpu.make_async_copy(
            rows.at[group], f_ref.at[:, :, pl.ds(pl.multiple_of(group * 128, 128), 128)], out_sem.at[i]
        )
        copy.start()
        outs.append(copy)

    for t in range(4):
        gr.wait(5, t)
        pass_r(6, t)
        gr.wait(6, t)
        pass_r(7, t)
    places = [(y, zl)] + [gr.received(i) for i in range(7)]
    for i, (p, w) in enumerate(places):
        write_out(w * 8 + p * 2 + k, i)
    for t in range(4):
        for i in range(8):
            r_sib[i, t].wait_recv()
    for i, (p, w) in enumerate(places):
        write_out(w * 8 + p * 2 + 1 - k, 8 + i)
    for t in range(4):
        rest(gf, t)

    unit = (lax.broadcasted_iota(jnp.int32, (128, 128), 0) == lax.broadcasted_iota(jnp.int32, (128, 128), 1))
    unit = unit.astype(jnp.bfloat16)

    def turn(block):
        turned[...] = lax.dot_general(
            unit, block.reshape(1024, 128), (((1,), (1,)), ((), ())), preferred_element_type=jnp.float32
        ).astype(jnp.bfloat16)

    def project(which):
        def to(place, group):
            def column(half):
                block = rows[group * 2 + half].reshape(1024, 128)
                return jnp.dot(turned[...], block, preferred_element_type=jnp.float32).astype(jnp.bfloat16)

            for half in range(2):
                place[:, half * 128:(half + 1) * 128] = column(half)

        copies = []
        for i, (xx, z) in enumerate(col_peers):
            group = xx * 2 + z
            to(part.at[which, group], group)
            copies.append(
                remote(part.at[which, group], parts.at[which, c], part_sems, which * 7 + i, col_device(xx, z))
            )
        to(parts.at[which, c], c)
        return copies

    turn(fs[pl.ds(c * 16, 16)])
    corr_copies = project(0)

    @pl.loop(0, 16)
    def _(column):
        image[column] = product(fs, column).astype(jnp.bfloat16)

    turn(image[...])
    proj_copies = project(1)

    for copy in corr_copies:
        copy.wait_recv()
    corr_ref[...] = jnp.sum(parts[0].astype(jnp.float32), axis=0) / 8192.0
    for copy in proj_copies:
        copy.wait_recv()
    proj_ref[...] = jnp.sum(parts[1].astype(jnp.float32), axis=0) / 8192.0
    for copy in outs:
        copy.wait()
    for copy in pending:
        copy.wait_send()


def shards(hamiltonian, block_cols, start_vectors):
    bf16, f32, dma = jnp.bfloat16, jnp.float32, pltpu.SemaphoreType.DMA
    vmem = pltpu.VMEM
    f, corr, proj = pl.pallas_call(
        kernel,
        out_shape=(
            jax.ShapeDtypeStruct((16, BLK, 2048), bf16),
            jax.ShapeDtypeStruct((128, 256), f32),
            jax.ShapeDtypeStruct((128, 256), f32),
        ),
        in_specs=[
            pl.BlockSpec(memory_space=pl.ANY),
            pl.BlockSpec(memory_space=pltpu.VMEM),
            pl.BlockSpec(memory_space=pl.ANY),
        ],
        out_specs=(
            pl.BlockSpec(memory_space=pl.ANY),
            pl.BlockSpec(memory_space=pltpu.VMEM),
            pl.BlockSpec(memory_space=pltpu.VMEM),
        ),
        scratch_shapes=[
            vmem((65, BLK, 128), bf16),
            vmem((8, 8, 128), jnp.int32),
            vmem((8, 128), jnp.int32),
            pltpu.SMEM((16, 128), jnp.int32),
            vmem((2, BLK, DEPTH), bf16),
            vmem((BLK, DEPTH), bf16),
            vmem((16, BLK, DEPTH), bf16),
            vmem((128, BLK, 128), bf16),
            vmem((128, BLK, 128), bf16),
            vmem((128, BLK, 128), bf16),
            vmem((16, 16, BLK, 128), bf16),
            vmem((16, BLK, 128), bf16),
            vmem((DEPTH, 128), bf16),
            vmem((128, 1024), bf16),
            vmem((2, 8, 128, 256), bf16),
            vmem((2, 8, 128, 256), bf16),
            dma((2,)),
            dma((2, 7)),
            dma((2, 7)),
            dma((2, 1)),
            dma((2,)),
            dma((2, 1)),
            dma((2, 7, 1)),
            dma((2, 8)),
            dma((2, 7, 1)),
            dma((2, 7, 4)),
            dma((2, 7, 4)),
            dma((2, 7, 4)),
            dma((2, 32)),
            dma((2, 14)),
            dma((16,)),
        ],
        compiler_params=pltpu.CompilerParams(
            collective_id=0, has_side_effects=True, vmem_limit_bytes=48 * 1024 * 1024
        ),
    )(hamiltonian.reshape(8, BLK, 1024), block_cols, start_vectors.reshape(16, BLK, 2048))
    return f.reshape(1024, 2048), corr, proj


def solution(mesh):
    in_specs = (P("row", "col"), P("row", None), P("col", None))
    out_specs = (P("col", None), P("row", "col"), P("row", "col"))
    return jax.shard_map(shards, mesh=mesh, in_specs=in_specs, out_specs=out_specs, check_vma=False)
```

```python
import jax
import jax.numpy as jnp
from jax import lax
from jax.experimental import pallas as pl
from jax.experimental.pallas import tpu as pltpu
from jax.sharding import PartitionSpec as P

BLK = 64
K_NB = 26
DEPTH = K_NB * BLK
MESH = pl.DeviceIdType.MESH
center_point = 0.2
half_width = 0.8


class Gather:
    def __init__(self, slot, p, w, pair, right, left, send_sem, recv_sem, pending):
        self.slot, self.p, self.w = slot, p, w
        self.pair, self.right, self.left = pair, right, left
        self.send_sem, self.recv_sem, self.pending = send_sem, recv_sem, pending

    def at(self, dp, dw):
        return lax.rem(self.p + dp + 4, 4), (self.w + dw) % 2

    def sent(self, i):
        return self.at(*((0, 0), (0, 0), (0, 0), (0, 1), (0, 1), (-1, 0), (1, 1))[i])

    def received(self, i):
        return self.at(*((0, 1), (-1, 0), (1, 0), (-1, 1), (1, 1), (2, 0), (2, 1))[i])

    def send(self, i, chunk=0, src=None):
        dst = self.slot(*self.sent(i), chunk)
        to = self.pair if i == 0 else (self.right if i % 2 else self.left)
        copy = pltpu.make_async_remote_copy(
            src_ref=dst if src is None else src,
            dst_ref=dst,
            send_sem=self.send_sem.at[i, chunk],
            recv_sem=self.recv_sem.at[i, chunk],
            device_id=to,
            device_id_type=MESH,
        )
        copy.start()
        self.pending.append(copy)

    def wait(self, i, chunk=0):
        ref = self.slot(*self.received(i), chunk)
        pltpu.make_async_remote_copy(
            src_ref=ref,
            dst_ref=ref,
            send_sem=self.send_sem.at[i, chunk],
            recv_sem=self.recv_sem.at[i, chunk],
            device_id=self.pair,
            device_id_type=MESH,
        ).wait_recv()


def kernel(
    h_ref, lists_ref, x_ref, f_ref, corr_ref, proj_ref,
    panels, lists, sib_list, index, halves, sib_half, packed, xs, ss, fs, rows, image, stack,
    own_lists, part, parts,
    own_sem, panel_sems, list_sems, sib_list_sem, index_sem, half_sem, h_sems, h_sib_sems,
    x_sems, s_sems, f_sems, r_sems, r_sib_sems, part_sems, out_sem,
):
    r = lax.axis_index("row")
    c = lax.axis_index("col")
    k = lax.rem(r, 2)
    chip = r // 2
    y = lax.rem(chip, 4)
    zl = r // 8
    x = c // 2
    zh = lax.rem(c, 2)
    sibling = (r + 1 - 2 * k, c)
    pending = []

    def ring(v, d):
        return lax.rem(v + d + 4, 4)

    def row_device(z, yy):
        return (z * 8 + yy * 2 + k, c)

    def col_device(xx, z):
        return (r, xx * 2 + z)

    def remote(src, dst, sems, i, to, start=True):
        copy = pltpu.make_async_remote_copy(
            src_ref=src, dst_ref=dst, send_sem=sems.at[0, i], recv_sem=sems.at[1, i],
            device_id=to, device_id_type=MESH,
        )
        if start:
            copy.start()
            pending.append(copy)
        return copy

    row_peers = [((zl + dz) % 2, ring(y, dy)) for dz in (1, 0) for dy in (0, 1, 3, 2) if dz or dy]
    col_peers = [(ring(x, dx), (zh + dw) % 2) for dw in (1, 0) for dx in (2, 1, 3, 0) if dw or dx]

    own_panel = pltpu.make_async_copy(
        h_ref.at[:, :, pl.ds(pl.multiple_of((2 * y + zl) * 128, 128), 128)],
        panels.at[pl.ds(chip * 8, 8)], own_sem.at[0],
    )
    own_panel.start()
    x_src = x_ref.at[:, :, pl.ds(pl.multiple_of(r * 128, 128), 128)]
    own_x = pltpu.make_async_copy(x_src, xs.at[pl.ds(c * 16, 16)], own_sem.at[1])
    own_x.start()
    read_lists = pltpu.make_async_copy(lists_ref, own_lists, own_sem.at[2])
    read_lists.start()
    read_lists.wait()
    lists[chip] = jnp.zeros((8, 128), jnp.int32)
    lists[chip, :, :K_NB] = own_lists[...]
    panels[64] = jnp.zeros((BLK, 128), jnp.bfloat16)

    barrier = pltpu.get_barrier_semaphore()
    for z, yy in row_peers:
        pl.semaphore_signal(barrier, inc=1, device_id=row_device(z, yy), device_id_type=MESH)
    for xx, z in col_peers:
        pl.semaphore_signal(barrier, inc=1, device_id=col_device(xx, z), device_id_type=MESH)
    across = (lax.rem(r + 8, 16), x * 2 + 1 - zh)
    for device in (sibling, across):
        pl.semaphore_signal(barrier, inc=1, device_id=device, device_id_type=MESH)
    pl.semaphore_wait(barrier, 16)

    list_copies, panel_copies = [], []
    for i, (z, yy) in enumerate(row_peers):
        list_copies.append(remote(lists.at[chip], lists.at[chip], list_sems, i, row_device(z, yy)))
    for i, (z, yy) in enumerate(row_peers):
        src = h_ref.at[:, :, pl.ds(pl.multiple_of((2 * yy + z) * 128, 128), 128)]
        panel_copies.append(remote(src, panels.at[pl.ds(chip * 8, 8)], panel_sems, i, row_device(z, yy)))

    def col_gather(buffer, sems, size, starts, pair):
        def slot(p, w, t):
            return buffer.at[pl.ds((p * 2 + w) * 16 + starts[t], size)]

        return Gather(slot, x, zh, pair, col_device(ring(x, 1), zh), col_device(ring(x, -1), zh),
                      sems.at[0], sems.at[1], pending)

    gx = col_gather(xs, x_sems, 16, (0,), across)
    x_across = x_ref.at[:, :, pl.ds(pl.multiple_of(lax.rem(r + 8, 16) * 128, 128), 128)]
    gx.send(0, 0, x_across)
    gx.send(1, 0, x_src)
    gx.send(2, 0, x_src)

    for copy in list_copies:
        copy.wait_recv()
    sib_lists = remote(lists.at[c], sib_list, sib_list_sem, 0, sibling)
    mine = pltpu.make_async_copy(lists.at[c], index.at[pl.ds(k * 8, 8)], index_sem.at[0])
    mine.start()
    sib_lists.wait_recv()
    theirs = pltpu.make_async_copy(sib_list, index.at[pl.ds((1 - k) * 8, 8)], index_sem.at[1])
    theirs.start()
    mine.wait()
    theirs.wait()

    own_x.wait()
    gx.wait(0)
    gx.send(3)
    gx.send(4)
    gx.wait(1)
    gx.send(5)

    own_panel.wait()
    for copy in panel_copies:
        copy.wait_recv()
    pair_column = 4 * y + 2 * zl
    lane = lax.broadcasted_iota(jnp.int32, (BLK, 128), 1)
    line = lax.broadcasted_iota(jnp.int32, (BLK, 128), 0)
    for side in range(2):
        for s in range(K_NB):
            i = index[pair_column + side, s]
            local = jnp.where(lax.rem(i // 8, 2) == k, 8 * (i // 16) + lax.rem(i, 8), 64)
            stack[s * BLK:(s + 1) * BLK, :] = panels[local]
        pick = (lane == line + BLK * side).astype(jnp.bfloat16)
        halves[side] = lax.dot_general(
            pick, stack[...], (((1,), (1,)), ((), ())), preferred_element_type=jnp.float32
        ).astype(jnp.bfloat16)
    swap = remote(halves.at[1 - k], sib_half, half_sem, 0, sibling)
    swap.wait_recv()
    packed[pair_column + k] = halves[k] + sib_half[...]

    def h_slot(p, w, t):
        return packed.at[p * 4 + w * 2 + k]

    def row_gather(slot, sems):
        return Gather(slot, y, zl, row_device(1 - zl, y), row_device(zl, ring(y, 1)), row_device(zl, ring(y, -1)),
                      sems.at[0], sems.at[1], pending)

    gh = row_gather(h_slot, h_sems)
    h_sib = {}

    def pass_h(i):
        slot = h_slot(y, zl, 0) if i == 0 else h_slot(*gh.received(i - 1), 0)
        h_sib[i] = remote(slot, slot, h_sib_sems, i, sibling)

    for i in range(3):
        gh.send(i)
    pass_h(0)

    gx.wait(4)
    gx.send(6)
    for i in (2, 3, 5, 6):
        gx.wait(i)

    def product(source, column):
        stacked = jnp.concatenate([source[index[column, s]] for s in range(K_NB)], axis=0)
        return jnp.dot(packed[column], stacked, preferred_element_type=jnp.float32)

    pairs = [gh.at(*d) for d in ((0, 0), (0, 1), (-1, 0), (1, 0), (1, 1), (-1, 1), (2, 0), (2, 1))]
    starts = [4 * p + 2 * w for p, w in pairs]
    across_z = col_device(x, 1 - zh)
    gs = col_gather(ss, s_sems, 2, starts, across_z)

    def first_degree(t, sib):
        h_sib[sib].wait_recv()
        for j in range(2):
            column = starts[t] + j
            at = c * 16 + column
            total = product(xs, column) - center_point * xs[at].astype(jnp.float32)
            ss[at] = (total / half_width).astype(jnp.bfloat16)
        for i in range(3):
            gs.send(i, t)

    def early(g, t):
        g.wait(1, t)
        g.send(5, t)
        g.wait(0, t)
        g.send(3, t)
        g.send(4, t)

    def late(g, t):
        g.wait(4, t)
        g.send(6, t)

    def rest(g, t):
        for i in (2, 3, 5, 6):
            g.wait(i, t)

    first_degree(0, 0)
    gh.wait(0)
    gh.send(3)
    gh.send(4)
    pass_h(1)
    gh.wait(1)
    gh.send(5)
    pass_h(2)
    gh.wait(2)
    pass_h(3)
    first_degree(1, 1)
    first_degree(2, 2)
    first_degree(3, 3)
    early(gs, 0)
    gh.wait(4)
    gh.send(6)
    pass_h(5)
    early(gs, 1)
    gh.wait(3)
    pass_h(4)
    early(gs, 2)
    early(gs, 3)
    first_degree(4, 5)
    first_degree(5, 4)
    late(gs, 0)
    late(gs, 1)
    gh.wait(5)
    pass_h(6)
    early(gs, 4)
    early(gs, 5)
    first_degree(6, 6)
    gh.wait(6)
    pass_h(7)
    late(gs, 2)
    late(gs, 3)
    early(gs, 6)
    first_degree(7, 7)
    late(gs, 4)
    late(gs, 5)
    late(gs, 6)
    early(gs, 7)
    late(gs, 7)
    for t in range(8):
        rest(gs, t)

    gf = col_gather(fs, f_sems, 4, (0, 4, 8, 12), across_z)

    def r_slot(parity):
        def slot(p, w, t):
            return rows.at[w * 8 + p * 2 + parity, pl.ds(4 * t, 4)]

        return slot

    gr = row_gather(r_slot(k), r_sems)
    r_sib = {}

    def pass_r(i):
        p, w = (y, zl) if i == 0 else gr.received(i - 1)
        slot = rows.at[w * 8 + p * 2 + k]
        r_sib[i] = remote(slot, slot, r_sib_sems, i, sibling)

    outs = []

    def write_out(group, i):
        copy = pltpu.make_async_copy(
            rows.at[group], f_ref.at[:, :, pl.ds(pl.multiple_of(group * 128, 128), 128)], out_sem.at[i]
        )
        copy.start()
        outs.append(copy)

    for t in range(4):
        for j in range(4):
            column = t * 4 + j
            at = c * 16 + column
            total = product(ss, column) - center_point * ss[at].astype(jnp.float32)
            out = ((2.0 / half_width) * total - xs[at].astype(jnp.float32)).astype(jnp.bfloat16)
            fs[at] = out
            rows[r, column] = out
        for i in (1, 2, 0):
            gf.send(i, t)
            gr.send(i, t)
    pass_r(0)
    for t in range(4):
        early(gr, t)
        early(gf, t)
    pass_r(1)
    pass_r(2)
    for t in range(4):
        gr.wait(2, t)
    pass_r(3)
    for t in range(4):
        late(gr, t)
        late(gf, t)
    pass_r(5)
    for t in range(4):
        gr.wait(3, t)
    pass_r(4)
    places = [(y, zl)] + [gr.received(i) for i in range(7)]
    for i, (p, w) in enumerate(places[:6]):
        write_out(w * 8 + p * 2 + k, i)
    for t in range(4):
        gr.wait(5, t)
    pass_r(6)
    for t in range(4):
        gr.wait(6, t)
    pass_r(7)
    for i in (6, 7):
        p, w = places[i]
        write_out(w * 8 + p * 2 + k, i)
    for i, (p, w) in enumerate(places):
        r_sib[i].wait_recv()
        write_out(w * 8 + p * 2 + 1 - k, 8 + i)

    def project(which, left):
        def to(place, group):
            for half in range(2):
                place[:, half * 128:(half + 1) * 128] = lax.dot_general(
                    left, rows[group * 2 + half].reshape(1024, 128), (((0,), (0,)), ((), ())),
                    preferred_element_type=jnp.float32,
                ).astype(jnp.bfloat16)

        copies = []
        for i, (xx, z) in enumerate(col_peers):
            group = xx * 2 + z
            to(part.at[which, group], group)
            copies.append(
                remote(part.at[which, group], parts.at[which, c], part_sems, which * 7 + i, col_device(xx, z))
            )
        to(parts.at[which, c], c)
        return copies

    corr_copies = project(0, fs[pl.ds(c * 16, 16)].reshape(1024, 128))
    for t in range(4):
        rest(gf, t)

    @pl.loop(0, 4)
    def _(j):
        for i in range(4):
            column = j * 4 + i
            image[column] = product(fs, column).astype(jnp.bfloat16)

    proj_copies = project(1, image[...].reshape(1024, 128))

    for copy in corr_copies:
        copy.wait_recv()
    corr_ref[...] = jnp.sum(parts[0].astype(jnp.float32), axis=0) / 8192.0
    for copy in proj_copies:
        copy.wait_recv()
    proj_ref[...] = jnp.sum(parts[1].astype(jnp.float32), axis=0) / 8192.0
    for copy in outs:
        copy.wait()
    for copy in pending:
        copy.wait_send()


def shards(hamiltonian, block_cols, start_vectors):
    bf16, f32, dma = jnp.bfloat16, jnp.float32, pltpu.SemaphoreType.DMA
    vmem = pltpu.VMEM
    place = pl.BlockSpec(memory_space=pl.ANY)
    out_shape = (
        jax.ShapeDtypeStruct((16, BLK, 2048), bf16),
        jax.ShapeDtypeStruct((128, 256), f32),
        jax.ShapeDtypeStruct((128, 256), f32),
    )
    results = pl.pallas_call(
        kernel,
        out_shape=out_shape,
        in_specs=[place] * 3,
        out_specs=(place, pl.BlockSpec(memory_space=pltpu.VMEM), pl.BlockSpec(memory_space=pltpu.VMEM)),
        scratch_shapes=[
            vmem((65, BLK, 128), bf16),
            vmem((8, 8, 128), jnp.int32),
            vmem((8, 128), jnp.int32),
            pltpu.SMEM((16, 128), jnp.int32),
            vmem((2, BLK, DEPTH), bf16),
            vmem((BLK, DEPTH), bf16),
            vmem((16, BLK, DEPTH), bf16),
            vmem((128, BLK, 128), bf16),
            vmem((128, BLK, 128), bf16),
            vmem((128, BLK, 128), bf16),
            vmem((16, 16, BLK, 128), bf16),
            vmem((16, BLK, 128), bf16),
            vmem((DEPTH, 128), bf16),
            vmem((8, K_NB), jnp.int32),
            vmem((2, 8, 128, 256), bf16),
            vmem((2, 8, 128, 256), bf16),
            dma((3,)),
            dma((2, 7)),
            dma((2, 7)),
            dma((2, 1)),
            dma((2,)),
            dma((2, 1)),
            dma((2, 7, 1)),
            dma((2, 8)),
            dma((2, 7, 1)),
            dma((2, 7, 8)),
            dma((2, 7, 4)),
            dma((2, 7, 4)),
            dma((2, 8)),
            dma((2, 14)),
            dma((16,)),
        ],
        compiler_params=pltpu.CompilerParams(
            collective_id=0, has_side_effects=True, vmem_limit_bytes=62 * 1024 * 1024
        ),
    )(hamiltonian.reshape(8, BLK, 1024), block_cols, start_vectors.reshape(16, BLK, 2048))

    def hand_on(*refs):
        sources, targets, sems = refs[:3], refs[3:6], refs[6]
        copies = [pltpu.make_async_copy(a.at[4 * i:4 * i + 4], b.at[4 * i:4 * i + 4], sems.at[i])
                  for a, b in (refs[0:4:3],) for i in range(4)]
        copies += [pltpu.make_async_copy(sources[i], targets[i], sems.at[3 + i]) for i in (1, 2)]
        for copy in copies:
            copy.start()
        for copy in copies:
            copy.wait()

    f, corr, proj = pl.pallas_call(
        hand_on,
        out_shape=out_shape,
        in_specs=[place] * 3,
        out_specs=(place,) * 3,
        scratch_shapes=[dma((6,))],
        compiler_params=pltpu.CompilerParams(vmem_limit_bytes=62 * 1024 * 1024),
    )(*results)
    return f.reshape(1024, 2048), corr, proj


def solution(mesh):
    in_specs = (P("row", "col"), P("row", None), P("col", None))
    out_specs = (P("col", None), P("row", "col"), P("row", "col"))
    return jax.shard_map(shards, mesh=mesh, in_specs=in_specs, out_specs=out_specs, check_vma=False)
```

```python
import jax
import jax.numpy as jnp
from jax import lax
from jax.experimental import pallas as pl
from jax.experimental.pallas import tpu as pltpu
from jax.sharding import PartitionSpec as P

BLK = 64
K_NB = 26
DEPTH = K_NB * BLK
MESH = pl.DeviceIdType.MESH
center_point = 0.2
half_width = 0.8

FIRST = (
    ("x", 5, 0), ("x", 3, 0), ("x", 4, 0), ("x", 5, 1), ("x", 3, 1), ("x", 4, 1), ("pack",), ("swap",), ("x", 6, 0),
    ("add",), ("h", 0, 0), ("h", 1, 0), ("h", 2, 0), ("p", 0, 0), ("h", 0, 1), ("h", 1, 1), ("h", 2, 1), ("p", 0, 1),
    ("x", 6, 1), ("h", 3, 0), ("h", 4, 0), ("p", 1, 0), ("h", 5, 0), ("p", 2, 0), ("p", 3, 0), ("h", 3, 1),
    ("h", 4, 1), ("p", 1, 1), ("h", 5, 1), ("p", 2, 1), ("p", 3, 1), ("s", 0), ("g", 5, 0), ("s", 1), ("g", 3, 0),
    ("g", 4, 0), ("p", 4, 0), ("h", 6, 0), ("p", 5, 0), ("s", 2), ("s", 3), ("p", 6, 0), ("h", 6, 1), ("p", 5, 1),
    ("g", 5, 1), ("g", 3, 1), ("g", 4, 1), ("g", 6, 0), ("g", 5, 2), ("s", 4), ("g", 3, 2), ("g", 4, 2), ("p", 4, 1),
    ("p", 7, 0), ("g", 5, 3), ("g", 3, 3), ("g", 4, 3), ("g", 6, 1), ("s", 5), ("g", 6, 2), ("p", 6, 1), ("p", 7, 1),
    ("g", 3, 4), ("g", 4, 4), ("g", 5, 4), ("s", 6), ("g", 6, 3), ("s", 7), ("g", 3, 5), ("g", 4, 5), ("g", 5, 5),
    ("g", 6, 4), ("g", 3, 6), ("g", 4, 6), ("g", 5, 6), ("g", 3, 7), ("g", 4, 7), ("g", 5, 7), ("g", 6, 5),
    ("g", 6, 6), ("g", 6, 7),
)
SECOND = (
    ("f", 0), ("f", 1), ("f", 2), ("f", 3), ("q", 0), ("r", 5, 0), ("r", 3, 0), ("r", 4, 0), ("a", 5, 0), ("a", 3, 0),
    ("a", 4, 0), ("r", 5, 1), ("r", 3, 1), ("r", 4, 1), ("a", 5, 1), ("a", 3, 1), ("a", 4, 1), ("r", 5, 2),
    ("r", 3, 2), ("r", 4, 2), ("a", 5, 2), ("a", 3, 2), ("a", 4, 2), ("r", 5, 3), ("r", 3, 3), ("r", 4, 3),
    ("a", 5, 3), ("a", 3, 3), ("a", 4, 3), ("q", 1), ("q", 2), ("q", 3), ("r", 6, 0), ("a", 6, 0), ("r", 6, 1),
    ("a", 6, 1), ("r", 6, 2), ("a", 6, 2), ("r", 6, 3), ("a", 6, 3), ("q", 5), ("q", 4), ("q", 6), ("q", 7),
)


class Gather:
    def __init__(self, slot, p, w, pair, right, left, send_sem, recv_sem, pending):
        self.slot, self.p, self.w = slot, p, w
        self.pair, self.right, self.left = pair, right, left
        self.send_sem, self.recv_sem, self.pending = send_sem, recv_sem, pending
        self.waited = set()

    def at(self, dp, dw):
        return lax.rem(self.p + dp + 4, 4), (self.w + dw) % 2

    def sent(self, i):
        return self.at(*((0, 0), (0, 0), (0, 0), (0, 1), (0, 1), (-1, 0), (1, 1))[i])

    def received(self, i):
        return self.at(*((0, 1), (-1, 0), (1, 0), (-1, 1), (1, 1), (2, 0), (2, 1))[i])

    def send(self, i, chunk=0, src=None):
        dst = self.slot(*self.sent(i), chunk)
        to = self.pair if i == 0 else (self.right if i % 2 else self.left)
        copy = pltpu.make_async_remote_copy(
            src_ref=dst if src is None else src,
            dst_ref=dst,
            send_sem=self.send_sem.at[i, chunk],
            recv_sem=self.recv_sem.at[i, chunk],
            device_id=to,
            device_id_type=MESH,
        )
        copy.start()
        self.pending.append(copy)

    def need(self, i, chunk=0):
        if (i, chunk) in self.waited:
            return
        self.waited.add((i, chunk))
        ref = self.slot(*self.received(i), chunk)
        pltpu.make_async_remote_copy(
            src_ref=ref,
            dst_ref=ref,
            send_sem=self.send_sem.at[i, chunk],
            recv_sem=self.recv_sem.at[i, chunk],
            device_id=self.pair,
            device_id_type=MESH,
        ).wait_recv()

    def step(self, i, chunk=0):
        if i >= 3:
            self.need((0, 0, 1, 4)[i - 3], chunk)
        self.send(i, chunk)


def kernel(
    h_ref, lists_ref, x_ref, f_ref, corr_ref, proj_ref,
    panels, lists, sib_list, index, halves, sib_half, packed, xs, ss, fs, rows, image,
    own_lists, part, parts,
    own_sem, panel_sems, list_sems, sib_list_sem, index_sem, half_sem, h_sems, h_sib_sems,
    x_sems, s_sems, f_sems, r_sems, r_sib_sems, part_sems, out_sem,
):
    r = lax.axis_index("row")
    c = lax.axis_index("col")
    k = lax.rem(r, 2)
    chip = r // 2
    y = lax.rem(chip, 4)
    zl = r // 8
    x = c // 2
    zh = lax.rem(c, 2)
    sibling = (r + 1 - 2 * k, c)
    pending = []

    def ring(v, d):
        return lax.rem(v + d + 4, 4)

    def row_device(z, yy):
        return (z * 8 + yy * 2 + k, c)

    def col_device(xx, z):
        return (r, xx * 2 + z)

    def remote(src, dst, sems, i, to, start=True):
        copy = pltpu.make_async_remote_copy(
            src_ref=src, dst_ref=dst, send_sem=sems.at[0, i], recv_sem=sems.at[1, i],
            device_id=to, device_id_type=MESH,
        )
        if start:
            copy.start()
            pending.append(copy)
        return copy

    row_peers = [((zl + dz) % 2, ring(y, dy)) for dz in (1, 0) for dy in (0, 1, 3, 2) if dz or dy]
    col_peers = [(ring(x, dx), (zh + dw) % 2) for dw in (1, 0) for dx in (2, 1, 3, 0) if dw or dx]

    own_panel = pltpu.make_async_copy(
        h_ref.at[:, :, pl.ds(pl.multiple_of((2 * y + zl) * 128, 128), 128)],
        panels.at[pl.ds(chip * 8, 8)], own_sem.at[0],
    )
    own_panel.start()
    x_src = x_ref.at[:, :, pl.ds(pl.multiple_of(r * 128, 128), 128)]
    own_x = pltpu.make_async_copy(x_src, xs.at[pl.ds(c * 16, 16)], own_sem.at[1])
    own_x.start()
    read_lists = pltpu.make_async_copy(lists_ref, own_lists, own_sem.at[2])
    read_lists.start()
    read_lists.wait()
    lists[chip] = jnp.zeros((8, 128), jnp.int32)
    lists[chip, :, :K_NB] = own_lists[...]
    panels[64] = jnp.zeros((BLK, 128), jnp.bfloat16)

    barrier = pltpu.get_barrier_semaphore()
    for z, yy in row_peers:
        pl.semaphore_signal(barrier, inc=1, device_id=row_device(z, yy), device_id_type=MESH)
    for xx, z in col_peers:
        pl.semaphore_signal(barrier, inc=1, device_id=col_device(xx, z), device_id_type=MESH)
    across = (lax.rem(r + 8, 16), x * 2 + 1 - zh)
    for device in (sibling, across):
        pl.semaphore_signal(barrier, inc=1, device_id=device, device_id_type=MESH)
    pl.semaphore_wait(barrier, 16)

    list_copies, panel_copies = [], []
    for i, (z, yy) in enumerate(row_peers):
        list_copies.append(remote(lists.at[chip], lists.at[chip], list_sems, i, row_device(z, yy)))
    def col_gather(buffer, sems, size, starts, pair):
        def slot(p, w, t):
            return buffer.at[pl.ds((p * 2 + w) * 16 + starts[t], size)]

        return Gather(slot, x, zh, pair, col_device(ring(x, 1), zh), col_device(ring(x, -1), zh),
                      sems.at[0], sems.at[1], pending)

    gx = col_gather(xs, x_sems, 8, (0, 8), across)
    x_across = x_ref.at[:, :, pl.ds(pl.multiple_of(lax.rem(r + 8, 16) * 128, 128), 128)]
    for t in range(2):
        for i in range(3):
            gx.send(i, t, (x_src if i else x_across).at[pl.ds(8 * t, 8)])

    for i, (z, yy) in enumerate(row_peers):
        src = h_ref.at[:, :, pl.ds(pl.multiple_of((2 * yy + z) * 128, 128), 128)]
        panel_copies.append(remote(src, panels.at[pl.ds(chip * 8, 8)], panel_sems, i, row_device(z, yy)))

    for copy in list_copies:
        copy.wait_recv()
    sib_lists = remote(lists.at[c], sib_list, sib_list_sem, 0, sibling)
    mine = pltpu.make_async_copy(lists.at[c], index.at[pl.ds(k * 8, 8)], index_sem.at[0])
    mine.start()
    sib_lists.wait_recv()
    theirs = pltpu.make_async_copy(sib_list, index.at[pl.ds((1 - k) * 8, 8)], index_sem.at[1])
    theirs.start()
    mine.wait()
    theirs.wait()

    pair_column = 4 * y + 2 * zl

    def pack():
        own_panel.wait()
        for copy in panel_copies:
            copy.wait_recv()
        lane = lax.broadcasted_iota(jnp.int32, (BLK, 128), 1)
        line = lax.broadcasted_iota(jnp.int32, (BLK, 128), 0)
        for side in range(2):
            blocks = []
            for s in range(K_NB):
                i = index[pair_column + side, s]
                blocks.append(panels[jnp.where(lax.rem(i // 8, 2) == k, 8 * (i // 16) + lax.rem(i, 8), 64)])
            pick = (lane == line + BLK * side).astype(jnp.bfloat16)
            halves[side] = lax.dot_general(
                pick, jnp.concatenate(blocks, axis=0), (((1,), (1,)), ((), ())), preferred_element_type=jnp.float32
            ).astype(jnp.bfloat16)

    swaps = []

    def swap():
        swaps.append(remote(halves.at[1 - k], sib_half, half_sem, 0, sibling))

    def add():
        swaps[0].wait_recv()
        packed[pair_column + k] = halves[k] + sib_half[...]

    def row_gather(slot, sems):
        return Gather(slot, y, zl, row_device(1 - zl, y), row_device(zl, ring(y, 1)), row_device(zl, ring(y, -1)),
                      sems.at[0], sems.at[1], pending)

    def h_slot(p, w, t):
        return packed.at[p * 4 + w * 2 + k, pl.ds(32 * t, 32)]

    gh = row_gather(h_slot, h_sems)
    h_sib = {}

    def pass_h(i, t):
        place = (y, zl)
        if i:
            gh.need(i - 1, t)
            place = gh.received(i - 1)
        slot = h_slot(*place, t)
        h_sib[i, t] = remote(slot, slot, h_sib_sems, 2 * i + t, sibling)

    def product(source, column):
        stacked = jnp.concatenate([source[index[column, s]] for s in range(K_NB)], axis=0)
        return jnp.dot(packed[column], stacked, preferred_element_type=jnp.float32)

    pairs = [gh.at(*d) for d in ((0, 0), (0, 1), (-1, 0), (1, 0), (1, 1), (-1, 1), (2, 0), (2, 1))]
    passes = (0, 1, 2, 3, 5, 4, 6, 7)
    starts = [4 * p + 2 * w for p, w in pairs]
    across_z = col_device(x, 1 - zh)
    gs = col_gather(ss, s_sems, 2, starts, across_z)

    def first_degree(u):
        if u == 0:
            own_x.wait()
            for t in range(2):
                for i in range(7):
                    gx.need(i, t)
        for t in range(2):
            if u:
                gh.need(passes[u] - 1, t)
            h_sib[passes[u], t].wait_recv()
        for j in range(2):
            column = starts[u] + j
            at = c * 16 + column
            total = product(xs, column) - center_point * xs[at].astype(jnp.float32)
            ss[at] = (total / half_width).astype(jnp.bfloat16)
        for i in range(3):
            gs.send(i, u)

    does = {"x": gx.step, "pack": pack, "swap": swap, "add": add, "h": gh.step, "p": pass_h, "s": first_degree,
            "g": gs.step}
    for name, *args in FIRST:
        does[name](*args)
    for t in range(8):
        for i in range(7):
            gs.need(i, t)

    gf = col_gather(fs, f_sems, 4, (0, 4, 8, 12), across_z)

    def r_slot(parity):
        def slot(p, w, t):
            return rows.at[w * 8 + p * 2 + parity, pl.ds(4 * t, 4)]

        return slot

    gr = row_gather(r_slot(k), r_sems)
    r_sib = {}

    outs = []

    def write_out(group):
        copy = pltpu.make_async_copy(
            rows.at[group], f_ref.at[:, :, pl.ds(pl.multiple_of(group * 128, 128), 128)], out_sem.at[len(outs)]
        )
        copy.start()
        outs.append(copy)

    def pass_r(i):
        place = (y, zl)
        if i:
            for t in range(4):
                gr.need(i - 1, t)
            place = gr.received(i - 1)
        p, w = place
        group = w * 8 + p * 2 + k
        r_sib[i] = remote(rows.at[group], rows.at[group], r_sib_sems, i, sibling)
        write_out(group)

    def second_degree(t):
        for j in range(4):
            column = t * 4 + j
            at = c * 16 + column
            total = product(ss, column) - center_point * ss[at].astype(jnp.float32)
            out = ((2.0 / half_width) * total - xs[at].astype(jnp.float32)).astype(jnp.bfloat16)
            fs[at] = out
            rows[r, column] = out
        for i in (1, 2, 0):
            gf.send(i, t)
            gr.send(i, t)

    does = {"f": second_degree, "a": gf.step, "r": gr.step, "q": pass_r}
    for name, *args in SECOND:
        does[name](*args)
    for i in range(8):
        p, w = gr.received(i - 1) if i else (y, zl)
        r_sib[i].wait_recv()
        write_out(w * 8 + p * 2 + 1 - k)

    def project(which, left):
        def to(place, group):
            for half in range(2):
                place[:, half * 128:(half + 1) * 128] = lax.dot_general(
                    left, rows[group * 2 + half].reshape(1024, 128), (((0,), (0,)), ((), ())),
                    preferred_element_type=jnp.float32,
                ).astype(jnp.bfloat16)

        copies = []
        for i, (xx, z) in enumerate(col_peers):
            group = xx * 2 + z
            to(part.at[which, group], group)
            copies.append(
                remote(part.at[which, group], parts.at[which, c], part_sems, which * 7 + i, col_device(xx, z))
            )
        to(parts.at[which, c], c)
        return copies

    corr_copies = project(0, fs[pl.ds(c * 16, 16)].reshape(1024, 128))
    for t in range(4):
        for i in range(7):
            gf.need(i, t)

    @pl.loop(0, 4)
    def _(j):
        for i in range(4):
            column = j * 4 + i
            image[column] = product(fs, column).astype(jnp.bfloat16)

    proj_copies = project(1, image[...].reshape(1024, 128))

    for copy in corr_copies:
        copy.wait_recv()
    corr_ref[...] = jnp.sum(parts[0].astype(jnp.float32), axis=0) / 8192.0
    for copy in proj_copies:
        copy.wait_recv()
    proj_ref[...] = jnp.sum(parts[1].astype(jnp.float32), axis=0) / 8192.0
    for copy in outs:
        copy.wait()
    for copy in pending:
        copy.wait_send()


def shards(hamiltonian, block_cols, start_vectors):
    bf16, f32, dma = jnp.bfloat16, jnp.float32, pltpu.SemaphoreType.DMA
    vmem = pltpu.VMEM
    place = pl.BlockSpec(memory_space=pl.ANY)
    out_shape = (
        jax.ShapeDtypeStruct((16, BLK, 2048), bf16),
        jax.ShapeDtypeStruct((128, 256), f32),
        jax.ShapeDtypeStruct((128, 256), f32),
    )
    results = pl.pallas_call(
        kernel,
        out_shape=out_shape,
        in_specs=[place] * 3,
        out_specs=(place, pl.BlockSpec(memory_space=pltpu.VMEM), pl.BlockSpec(memory_space=pltpu.VMEM)),
        scratch_shapes=[
            vmem((65, BLK, 128), bf16),
            vmem((8, 8, 128), jnp.int32),
            vmem((8, 128), jnp.int32),
            pltpu.SMEM((16, 128), jnp.int32),
            vmem((2, BLK, DEPTH), bf16),
            vmem((BLK, DEPTH), bf16),
            vmem((16, BLK, DEPTH), bf16),
            vmem((128, BLK, 128), bf16),
            vmem((128, BLK, 128), bf16),
            vmem((128, BLK, 128), bf16),
            vmem((16, 16, BLK, 128), bf16),
            vmem((16, BLK, 128), bf16),
            vmem((8, K_NB), jnp.int32),
            vmem((2, 8, 128, 256), bf16),
            vmem((2, 8, 128, 256), bf16),
            dma((3,)),
            dma((2, 7)),
            dma((2, 7)),
            dma((2, 1)),
            dma((2,)),
            dma((2, 1)),
            dma((2, 7, 2)),
            dma((2, 16)),
            dma((2, 7, 2)),
            dma((2, 7, 8)),
            dma((2, 7, 4)),
            dma((2, 7, 4)),
            dma((2, 8)),
            dma((2, 14)),
            dma((16,)),
        ],
        compiler_params=pltpu.CompilerParams(
            collective_id=0, has_side_effects=True, vmem_limit_bytes=48 * 1024 * 1024
        ),
    )(hamiltonian.reshape(8, BLK, 1024), block_cols, start_vectors.reshape(16, BLK, 2048))

    def hand_on(*refs):
        copies = [pltpu.make_async_copy(refs[i], refs[3 + i], refs[6].at[i]) for i in range(3)]
        for copy in copies:
            copy.start()
        for copy in copies:
            copy.wait()

    f, corr, proj = pl.pallas_call(
        hand_on,
        out_shape=out_shape,
        in_specs=[place] * 3,
        out_specs=(place,) * 3,
        scratch_shapes=[dma((3,))],
        compiler_params=pltpu.CompilerParams(vmem_limit_bytes=40 * 1024 * 1024),
    )(*results)
    return f.reshape(1024, 2048), corr, proj


def solution(mesh):
    in_specs = (P("row", "col"), P("row", None), P("col", None))
    out_specs = (P("col", None), P("row", "col"), P("row", "col"))
    return jax.shard_map(shards, mesh=mesh, in_specs=in_specs, out_specs=out_specs, check_vma=False)
```

```python
import jax
import jax.numpy as jnp
from jax import lax
from jax.experimental import pallas as pl
from jax.experimental.pallas import tpu as pltpu
from jax.sharding import PartitionSpec as P

BLK = 64
K_NB = 26
DEPTH = K_NB * BLK
MESH = pl.DeviceIdType.MESH
center_point = 0.2
half_width = 0.8

FORWARD = (((0, 0), "P"), ((0, 0), "R"), ((0, 0), "L"), ((0, 1), "R"),
           ((0, 1), "L"), ((-1, 0), "R"), ((1, 1), "L"))
PAIR_LAST_RIGHT = (((0, 0), "P"), ((0, 0), "R"), ((0, 0), "L"), ((-1, 0), "P"),
                   ((1, 0), "P"), ((-1, 0), "R"), ((2, 0), "P"))
PAIR_LAST_DIRECT = (((0, 0), "P"), ((0, 0), "R"), ((0, 0), "L"), ((-1, 0), "P"),
                    ((1, 0), "P"), ((0, 0), "X"), ((2, 0), "P"))
DIRECT = (((0, 0), "P"), ((0, 0), "R"), ((0, 0), "L"), ((0, 1), "R"),
          ((0, 1), "L"), ((0, 0), "X"), ((0, 1), "X"))
S_MESSAGES = (DIRECT, FORWARD, PAIR_LAST_DIRECT, FORWARD, PAIR_LAST_RIGHT, FORWARD, PAIR_LAST_DIRECT, DIRECT)
F_MESSAGES = (FORWARD, FORWARD, FORWARD, FORWARD)
ROW_MESSAGES = (FORWARD, FORWARD, FORWARD, FORWARD)
SLOTS = ((0, 0), (0, 1), (-1, 0), (1, 0), (-1, 1), (1, 1), (2, 0), (2, 1))
FIRST = (
    ("x", 5, 0), ("x", 3, 0), ("x", 4, 0), ("x", 5, 1), ("x", 3, 1), ("x", 4, 1), ("pack",), ("x", 6, 0), ("add",),
    ("h", 0, 0), ("h", 1, 0), ("h", 2, 0), ("p", 0, 0), ("h", 0, 1), ("h", 1, 1), ("h", 2, 1), ("p", 0, 1),
    ("x", 6, 1), ("h", 3, 0), ("h", 4, 0), ("p", 1, 0), ("h", 5, 0), ("p", 2, 0), ("p", 3, 0), ("h", 3, 1),
    ("h", 4, 1), ("p", 1, 1), ("h", 5, 1), ("p", 2, 1), ("p", 3, 1), ("s", 0), ("s", 1), ("g", 3, 0), ("g", 4, 0),
    ("p", 4, 0), ("h", 6, 0), ("p", 5, 0), ("g", 6, 0), ("s", 2), ("s", 3), ("g", 5, 1), ("p", 6, 0), ("h", 6, 1),
    ("p", 5, 1), ("g", 3, 1), ("g", 4, 1), ("s", 4), ("g", 3, 2), ("p", 4, 1), ("p", 7, 0), ("g", 4, 2), ("g", 3, 3),
    ("g", 4, 3), ("g", 6, 2), ("g", 5, 3), ("s", 5), ("g", 6, 1), ("p", 6, 1), ("p", 7, 1), ("g", 4, 4), ("g", 6, 3),
    ("g", 3, 4), ("g", 5, 4), ("s", 6), ("s", 7), ("g", 5, 5), ("g", 3, 5), ("g", 4, 5), ("g", 6, 4), ("g", 4, 6),
    ("g", 3, 6), ("g", 6, 6), ("g", 3, 7), ("g", 4, 7), ("g", 6, 7), ("g", 6, 5),
)
SECOND = (
    ("f", 0), ("f", 1), ("f", 2), ("f", 3), ("q", 0), ("r", 5, 0), ("r", 3, 0), ("r", 4, 0), ("a", 5, 0), ("a", 3, 0),
    ("a", 4, 0), ("r", 5, 1), ("r", 3, 1), ("r", 4, 1), ("a", 5, 1), ("a", 3, 1), ("a", 4, 1), ("r", 5, 2),
    ("r", 3, 2), ("r", 4, 2), ("a", 5, 2), ("a", 3, 2), ("a", 4, 2), ("r", 5, 3), ("r", 3, 3), ("r", 4, 3),
    ("a", 5, 3), ("a", 3, 3), ("a", 4, 3), ("q", 1), ("q", 2), ("q", 3), ("r", 6, 0), ("a", 6, 0), ("r", 6, 1),
    ("a", 6, 1), ("r", 6, 2), ("a", 6, 2), ("r", 6, 3), ("a", 6, 3), ("q", 5), ("q", 4), ("q", 6), ("q", 7),
)


def same(slot):
    return slot[0] % 4, slot[1] % 2


def comes(message):
    (dp, dw), to = message
    return same({"P": (dp, dw + 1), "R": (dp - 1, dw), "L": (dp + 1, dw), "X": (dp + 2, dw)}[to])


class Gather:
    def __init__(self, slot, p, w, devices, sems, pending, messages):
        self.slot, self.p, self.w, self.devices = slot, p, w, devices
        self.send_sem, self.recv_sem, self.pending = sems.at[0], sems.at[1], pending
        self.messages = messages
        self.waited = set()

    def at(self, dp, dw):
        return lax.rem(self.p + dp + 4, 4), (self.w + dw) % 2

    def copy(self, ref, src, i, chunk):
        return pltpu.make_async_remote_copy(
            src_ref=src,
            dst_ref=ref,
            send_sem=self.send_sem.at[i, chunk],
            recv_sem=self.recv_sem.at[i, chunk],
            device_id=self.devices[self.messages[chunk][i][1]],
            device_id_type=MESH,
        )

    def carrier(self, slot, chunk):
        brings = [comes(message) for message in self.messages[chunk]]
        return None if same(slot) == (0, 0) else brings.index(same(slot))

    def need(self, slot, chunk=0):
        i = self.carrier(slot, chunk)
        if i is not None and (i, chunk) not in self.waited:
            self.waited.add((i, chunk))
            ref = self.slot(*self.at(*slot), chunk)
            self.copy(ref, ref, i, chunk).wait_recv()
        return self.at(*slot)

    def need_all(self):
        for chunk in range(len(self.messages)):
            for slot in SLOTS:
                self.need(slot, chunk)

    def own(self, chunk=0, sources=None):
        for i, (slot, to) in enumerate(self.messages[chunk]):
            if slot == (0, 0):
                self.step(i, chunk, sources and sources[to])

    def step(self, i, chunk=0, src=None):
        dst = self.slot(*self.need(self.messages[chunk][i][0], chunk), chunk)
        copy = self.copy(dst, dst if src is None else src, i, chunk)
        copy.start()
        self.pending.append(copy)


def kernel(
    h_ref, lists_ref, x_ref, f_ref, corr_ref, proj_ref,
    panels, lists, sib_list, index, halves, sib_half, packed, xs, ss, fs, rows, image,
    own_lists, part, parts,
    own_sem, panel_sems, list_sems, sib_list_sem, index_sem, half_sem, h_sems, h_sib_sems,
    x_sems, s_sems, f_sems, r_sems, r_sib_sems, part_sems, out_sem,
):
    r = lax.axis_index("row")
    c = lax.axis_index("col")
    k = lax.rem(r, 2)
    chip = r // 2
    y = lax.rem(chip, 4)
    zl = r // 8
    x = c // 2
    zh = lax.rem(c, 2)
    sibling = (r + 1 - 2 * k, c)
    pending = []

    def ring(v, d):
        return lax.rem(v + d + 4, 4)

    def row_device(z, yy):
        return (z * 8 + yy * 2 + k, c)

    def col_device(xx, z):
        return (r, xx * 2 + z)

    def remote(src, dst, sems, i, to, start=True):
        copy = pltpu.make_async_remote_copy(
            src_ref=src, dst_ref=dst, send_sem=sems.at[0, i], recv_sem=sems.at[1, i],
            device_id=to, device_id_type=MESH,
        )
        if start:
            copy.start()
            pending.append(copy)
        return copy

    row_peers = [((zl + dz) % 2, ring(y, dy)) for dz in (1, 0) for dy in (0, 1, 3, 2) if dz or dy]
    col_peers = [(ring(x, dx), (zh + dw) % 2) for dw in (1, 0) for dx in (2, 1, 3, 0) if dw or dx]

    own_panel = pltpu.make_async_copy(
        h_ref.at[:, :, pl.ds(pl.multiple_of((2 * y + zl) * 128, 128), 128)],
        panels.at[pl.ds(chip * 8, 8)], own_sem.at[0],
    )
    own_panel.start()
    x_src = x_ref.at[:, :, pl.ds(pl.multiple_of(r * 128, 128), 128)]
    own_x = pltpu.make_async_copy(x_src, xs.at[pl.ds(c * 16, 16)], own_sem.at[1])
    own_x.start()
    read_lists = pltpu.make_async_copy(lists_ref, own_lists, own_sem.at[2])
    read_lists.start()
    panels[64] = jnp.zeros((BLK, 128), jnp.bfloat16)

    barrier = pltpu.get_barrier_semaphore()
    for z, yy in row_peers:
        pl.semaphore_signal(barrier, inc=1, device_id=row_device(z, yy), device_id_type=MESH)
    for xx, z in col_peers:
        pl.semaphore_signal(barrier, inc=1, device_id=col_device(xx, z), device_id_type=MESH)
    across = (lax.rem(r + 8, 16), x * 2 + 1 - zh)
    for device in (sibling, across):
        pl.semaphore_signal(barrier, inc=1, device_id=device, device_id_type=MESH)
    read_lists.wait()
    lists[chip] = jnp.zeros((8, 128), jnp.int32)
    lists[chip, :, :K_NB] = own_lists[...]
    pl.semaphore_wait(barrier, 16)

    list_copies, panel_copies = [], []
    for i, (z, yy) in enumerate(row_peers):
        list_copies.append(remote(lists.at[chip], lists.at[chip], list_sems, i, row_device(z, yy)))
    def col_gather(buffer, sems, size, starts, pair, messages):
        def slot(p, w, t):
            return buffer.at[pl.ds((p * 2 + w) * 16 + starts[t], size)]

        devices = {"P": pair, "R": col_device(ring(x, 1), zh), "L": col_device(ring(x, -1), zh),
                   "X": col_device(ring(x, 2), zh)}
        return Gather(slot, x, zh, devices, sems, pending, messages)

    gx = col_gather(xs, x_sems, 8, (0, 8), across, (FORWARD,) * 2)
    x_across = x_ref.at[:, :, pl.ds(pl.multiple_of(lax.rem(r + 8, 16) * 128, 128), 128)]
    for t in range(2):
        half = pl.ds(8 * t, 8)
        gx.own(t, {"P": x_across.at[half], "R": x_src.at[half], "L": x_src.at[half]})

    for i, (z, yy) in enumerate(row_peers):
        src = h_ref.at[:, :, pl.ds(pl.multiple_of((2 * yy + z) * 128, 128), 128)]
        panel_copies.append(remote(src, panels.at[pl.ds(chip * 8, 8)], panel_sems, i, row_device(z, yy)))

    for copy in list_copies:
        copy.wait_recv()
    sib_lists = remote(lists.at[c], sib_list, sib_list_sem, 0, sibling)
    mine = pltpu.make_async_copy(lists.at[c], index.at[pl.ds(k * 8, 8)], index_sem.at[0])
    mine.start()
    sib_lists.wait_recv()
    theirs = pltpu.make_async_copy(sib_list, index.at[pl.ds((1 - k) * 8, 8)], index_sem.at[1])
    theirs.start()
    mine.wait()
    theirs.wait()

    pair_column = 4 * y + 2 * zl

    def pack_side(side):
        lane = lax.broadcasted_iota(jnp.int32, (BLK, 128), 1)
        line = lax.broadcasted_iota(jnp.int32, (BLK, 128), 0)
        blocks = []
        for s in range(K_NB):
            i = index[pair_column + side, s]
            blocks.append(panels[jnp.where(lax.rem(i // 8, 2) == k, 8 * (i // 16) + lax.rem(i, 8), 64)])
        pick = (lane == line + BLK * side).astype(jnp.bfloat16)
        return lax.dot_general(
            pick, jnp.concatenate(blocks, axis=0), (((1,), (1,)), ((), ())), preferred_element_type=jnp.float32
        ).astype(jnp.bfloat16)

    swaps = []

    def pack():
        own_panel.wait()
        for copy in panel_copies:
            copy.wait_recv()
        halves[0] = pack_side(1 - k)
        swaps.append(remote(halves.at[0], sib_half, half_sem, 0, sibling))
        halves[1] = pack_side(k)

    def add():
        swaps[0].wait_recv()
        packed[pair_column + k] = halves[1] + sib_half[...]

    def row_gather(slot, sems, messages):
        devices = {"P": row_device(1 - zl, y), "R": row_device(zl, ring(y, 1)), "L": row_device(zl, ring(y, -1)),
                   "X": row_device(zl, ring(y, 2))}
        return Gather(slot, y, zl, devices, sems, pending, messages)

    def h_slot(p, w, t):
        return packed.at[p * 4 + w * 2 + k, pl.ds(32 * t, 32)]

    gh = row_gather(h_slot, h_sems, (FORWARD,) * 2)
    h_sib = {}

    def pass_h(i, t):
        slot = h_slot(*gh.need(SLOTS[i], t), t)
        h_sib[i, t] = remote(slot, slot, h_sib_sems, 2 * i + t, sibling)

    def product(source, column):
        stacked = jnp.concatenate([source[index[column, s]] for s in range(K_NB)], axis=0)
        return jnp.dot(packed[column], stacked, preferred_element_type=jnp.float32)

    passes = (0, 1, 2, 3, 5, 4, 6, 7)
    starts = [4 * p + 2 * w for p, w in (gh.at(*SLOTS[i]) for i in passes)]
    across_z = col_device(x, 1 - zh)
    gs = col_gather(ss, s_sems, 2, starts, across_z, S_MESSAGES)

    def first_degree(u):
        if u == 0:
            own_x.wait()
            gx.need_all()
        for t in range(2):
            gh.need(SLOTS[passes[u]], t)
            h_sib[passes[u], t].wait_recv()
        for j in range(2):
            column = starts[u] + j
            at = c * 16 + column
            total = product(xs, column) - center_point * xs[at].astype(jnp.float32)
            ss[at] = (total / half_width).astype(jnp.bfloat16)
        gs.own(u)

    does = {"x": gx.step, "pack": pack, "add": add, "h": gh.step, "p": pass_h, "s": first_degree,
            "g": gs.step}
    for name, *args in FIRST:
        does[name](*args)
    gs.need_all()

    gf = col_gather(fs, f_sems, 4, (0, 4, 8, 12), across_z, F_MESSAGES)

    def r_slot(parity):
        def slot(p, w, t):
            return rows.at[w * 8 + p * 2 + parity, pl.ds(4 * t, 4)]

        return slot

    gr = row_gather(r_slot(k), r_sems, ROW_MESSAGES)
    r_sib = {}

    outs = []

    def write_out(group):
        copy = pltpu.make_async_copy(
            rows.at[group], f_ref.at[:, :, pl.ds(pl.multiple_of(group * 128, 128), 128)], out_sem.at[len(outs)]
        )
        copy.start()
        outs.append(copy)

    def pass_r(i):
        for t in range(4):
            p, w = gr.need(SLOTS[i], t)
        group = w * 8 + p * 2 + k
        r_sib[i] = remote(rows.at[group], rows.at[group], r_sib_sems, i, sibling)
        write_out(group)

    def second_degree(t):
        for j in range(4):
            column = t * 4 + j
            at = c * 16 + column
            total = product(ss, column) - center_point * ss[at].astype(jnp.float32)
            out = ((2.0 / half_width) * total - xs[at].astype(jnp.float32)).astype(jnp.bfloat16)
            fs[at] = out
            rows[r, column] = out
        gf.own(t)
        gr.own(t)

    does = {"f": second_degree, "a": gf.step, "r": gr.step, "q": pass_r}
    for name, *args in SECOND:
        does[name](*args)
    for i in range(8):
        p, w = gr.at(*SLOTS[i])
        r_sib[i].wait_recv()
        write_out(w * 8 + p * 2 + 1 - k)

    def project(which, left):
        def to(place, group):
            for half in range(2):
                place[:, half * 128:(half + 1) * 128] = lax.dot_general(
                    left, rows[group * 2 + half].reshape(1024, 128), (((0,), (0,)), ((), ())),
                    preferred_element_type=jnp.float32,
                ).astype(jnp.bfloat16)

        copies = []
        for i, (xx, z) in enumerate(col_peers):
            group = xx * 2 + z
            to(part.at[which, group], group)
            copies.append(
                remote(part.at[which, group], parts.at[which, c], part_sems, which * 7 + i, col_device(xx, z))
            )
        to(parts.at[which, c], c)
        return copies

    corr_copies = project(0, fs[pl.ds(c * 16, 16)].reshape(1024, 128))
    gf.need_all()

    @pl.loop(0, 4)
    def _(j):
        for i in range(4):
            column = j * 4 + i
            image[column] = product(fs, column).astype(jnp.bfloat16)

    proj_copies = project(1, image[...].reshape(1024, 128))

    for copy in pending[:-14]:
        copy.wait_send()
    for copy in outs:
        copy.wait()
    for copy in corr_copies:
        copy.wait_recv()
    corr_ref[...] = jnp.sum(parts[0].astype(jnp.float32), axis=0) / 8192.0
    for copy in proj_copies:
        copy.wait_recv()
    proj_ref[...] = jnp.sum(parts[1].astype(jnp.float32), axis=0) / 8192.0
    for copy in corr_copies + proj_copies:
        copy.wait_send()


def shards(hamiltonian, block_cols, start_vectors):
    bf16, f32, dma = jnp.bfloat16, jnp.float32, pltpu.SemaphoreType.DMA
    vmem = pltpu.VMEM
    place = pl.BlockSpec(memory_space=pl.ANY)
    out_shape = (
        jax.ShapeDtypeStruct((16, BLK, 2048), bf16),
        jax.ShapeDtypeStruct((128, 256), f32),
        jax.ShapeDtypeStruct((128, 256), f32),
    )
    results = pl.pallas_call(
        kernel,
        out_shape=out_shape,
        in_specs=[place] * 3,
        out_specs=(place, pl.BlockSpec(memory_space=pltpu.VMEM), pl.BlockSpec(memory_space=pltpu.VMEM)),
        scratch_shapes=[
            vmem((65, BLK, 128), bf16),
            vmem((8, 8, 128), jnp.int32),
            vmem((8, 128), jnp.int32),
            pltpu.SMEM((16, 128), jnp.int32),
            vmem((2, BLK, DEPTH), bf16),
            vmem((BLK, DEPTH), bf16),
            vmem((16, BLK, DEPTH), bf16),
            vmem((128, BLK, 128), bf16),
            vmem((128, BLK, 128), bf16),
            vmem((128, BLK, 128), bf16),
            vmem((16, 16, BLK, 128), bf16),
            vmem((16, BLK, 128), bf16),
            vmem((8, K_NB), jnp.int32),
            vmem((2, 8, 128, 256), bf16),
            vmem((2, 8, 128, 256), bf16),
            dma((3,)),
            dma((2, 7)),
            dma((2, 7)),
            dma((2, 1)),
            dma((2,)),
            dma((2, 1)),
            dma((2, 7, 2)),
            dma((2, 16)),
            dma((2, 7, 2)),
            dma((2, 7, 8)),
            dma((2, 7, 4)),
            dma((2, 7, 4)),
            dma((2, 8)),
            dma((2, 14)),
            dma((16,)),
        ],
        compiler_params=pltpu.CompilerParams(
            collective_id=0, has_side_effects=True, vmem_limit_bytes=48 * 1024 * 1024
        ),
    )(hamiltonian.reshape(8, BLK, 1024), block_cols, start_vectors.reshape(16, BLK, 2048))

    def hand_on(*refs):
        copies = [pltpu.make_async_copy(refs[i], refs[3 + i], refs[6].at[i]) for i in (1, 2)]
        for i in range(4):
            part = pl.ds(4 * i, 4)
            copies.append(pltpu.make_async_copy(refs[0].at[part], refs[3].at[part], refs[6].at[3 + i]))
        for copy in copies:
            copy.start()
        for copy in copies:
            copy.wait()

    f, corr, proj = pl.pallas_call(
        hand_on,
        out_shape=out_shape,
        in_specs=[place] * 3,
        out_specs=(place,) * 3,
        scratch_shapes=[dma((7,))],
        compiler_params=pltpu.CompilerParams(vmem_limit_bytes=40 * 1024 * 1024),
    )(*results)
    return f.reshape(1024, 2048), corr, proj


def solution(mesh):
    in_specs = (P("row", "col"), P("row", None), P("col", None))
    out_specs = (P("col", None), P("row", "col"), P("row", "col"))
    return jax.shard_map(shards, mesh=mesh, in_specs=in_specs, out_specs=out_specs, check_vma=False)
```

```python
import jax
import jax.numpy as jnp
from jax import lax
from jax.experimental import pallas as pl
from jax.experimental.pallas import tpu as pltpu
from jax.sharding import PartitionSpec as P

BLK = 64
K_NB = 26
DEPTH = K_NB * BLK
MESH = pl.DeviceIdType.MESH
center_point = 0.2
half_width = 0.8

FORWARD = (((0, 0), "P"), ((0, 0), "R"), ((0, 0), "L"), ((0, 1), "R"),
           ((0, 1), "L"), ((-1, 0), "R"), ((1, 1), "L"))
PAIR_LAST_RIGHT = (((0, 0), "P"), ((0, 0), "R"), ((0, 0), "L"), ((-1, 0), "P"),
                   ((1, 0), "P"), ((-1, 0), "R"), ((2, 0), "P"))
PAIR_LAST_LEFT = (((0, 0), "P"), ((0, 0), "R"), ((0, 0), "L"), ((-1, 0), "P"),
                  ((1, 0), "P"), ((1, 0), "L"), ((2, 0), "P"))
PAIR_LAST_DIRECT = (((0, 0), "P"), ((0, 0), "R"), ((0, 0), "L"), ((-1, 0), "P"),
                    ((1, 0), "P"), ((0, 0), "X"), ((2, 0), "P"))
DIRECT = (((0, 0), "P"), ((0, 0), "R"), ((0, 0), "L"), ((0, 1), "R"),
          ((0, 1), "L"), ((0, 0), "X"), ((0, 1), "X"))
S_MESSAGES = (DIRECT, PAIR_LAST_LEFT, PAIR_LAST_LEFT, FORWARD, PAIR_LAST_RIGHT, FORWARD, PAIR_LAST_DIRECT, DIRECT)
F_MESSAGES = (FORWARD, FORWARD, FORWARD, FORWARD)
ROW_MESSAGES = (FORWARD, FORWARD, FORWARD, FORWARD)
SLOTS = ((0, 0), (0, 1), (-1, 0), (1, 0), (-1, 1), (1, 1), (2, 0), (2, 1))
FIRST = (
    ("x", 5, 0), ("x", 3, 0), ("x", 4, 0), ("x", 5, 1), ("x", 3, 1), ("x", 4, 1), ("pack",), ("x", 6, 0), ("add",),
    ("h", 0, 0), ("h", 1, 0), ("h", 2, 0), ("p", 0, 0), ("h", 0, 1), ("h", 1, 1), ("h", 2, 1), ("p", 0, 1),
    ("x", 6, 1), ("h", 3, 0), ("h", 4, 0), ("p", 1, 0), ("h", 5, 0), ("p", 2, 0), ("p", 3, 0), ("h", 3, 1),
    ("h", 4, 1), ("p", 1, 1), ("h", 5, 1), ("p", 2, 1), ("p", 3, 1), ("s", 0), ("s", 1), ("g", 3, 0), ("g", 4, 0),
    ("p", 4, 0), ("h", 6, 0), ("p", 5, 0), ("g", 6, 0), ("s", 2), ("s", 3), ("g", 3, 1), ("g", 4, 1), ("p", 6, 0),
    ("h", 6, 1), ("p", 5, 1), ("g", 5, 1), ("s", 4), ("g", 3, 2), ("p", 4, 1), ("p", 7, 0), ("g", 4, 2), ("g", 5, 2),
    ("g", 3, 3), ("g", 4, 3), ("g", 5, 3), ("g", 6, 1), ("s", 5), ("p", 6, 1), ("g", 3, 4), ("p", 7, 1), ("g", 5, 4),
    ("g", 4, 4), ("g", 6, 2), ("s", 6), ("g", 6, 3), ("s", 7), ("g", 5, 5), ("g", 6, 4), ("g", 3, 5), ("g", 4, 5),
    ("g", 3, 6), ("g", 4, 6), ("g", 6, 6), ("g", 3, 7), ("g", 4, 7), ("g", 6, 7), ("g", 6, 5),
)
SECOND = (
    ("f", 0), ("f", 1), ("f", 2), ("f", 3), ("q", 0), ("r", 5, 0), ("r", 3, 0), ("r", 4, 0), ("a", 5, 0), ("a", 3, 0),
    ("a", 4, 0), ("r", 5, 1), ("r", 3, 1), ("r", 4, 1), ("a", 5, 1), ("a", 3, 1), ("a", 4, 1), ("r", 5, 2),
    ("r", 3, 2), ("r", 4, 2), ("a", 5, 2), ("a", 3, 2), ("a", 4, 2), ("r", 5, 3), ("r", 3, 3), ("r", 4, 3),
    ("a", 5, 3), ("a", 3, 3), ("a", 4, 3), ("q", 1), ("q", 2), ("q", 3), ("r", 6, 0), ("a", 6, 0), ("r", 6, 1),
    ("a", 6, 1), ("r", 6, 2), ("a", 6, 2), ("r", 6, 3), ("a", 6, 3), ("q", 5), ("q", 4), ("q", 6), ("q", 7),
)


def same(slot):
    return slot[0] % 4, slot[1] % 2


def comes(message):
    (dp, dw), to = message
    return same({"P": (dp, dw + 1), "R": (dp - 1, dw), "L": (dp + 1, dw), "X": (dp + 2, dw)}[to])


class Gather:
    def __init__(self, slot, p, w, devices, sems, pending, messages):
        self.slot, self.p, self.w, self.devices = slot, p, w, devices
        self.send_sem, self.recv_sem, self.pending = sems.at[0], sems.at[1], pending
        self.messages = messages
        self.waited = set()

    def at(self, dp, dw):
        return lax.rem(self.p + dp + 4, 4), (self.w + dw) % 2

    def copy(self, ref, src, i, chunk):
        return pltpu.make_async_remote_copy(
            src_ref=src,
            dst_ref=ref,
            send_sem=self.send_sem.at[i, chunk],
            recv_sem=self.recv_sem.at[i, chunk],
            device_id=self.devices[self.messages[chunk][i][1]],
            device_id_type=MESH,
        )

    def carrier(self, slot, chunk):
        brings = [comes(message) for message in self.messages[chunk]]
        return None if same(slot) == (0, 0) else brings.index(same(slot))

    def need(self, slot, chunk=0):
        i = self.carrier(slot, chunk)
        if i is not None and (i, chunk) not in self.waited:
            self.waited.add((i, chunk))
            ref = self.slot(*self.at(*slot), chunk)
            self.copy(ref, ref, i, chunk).wait_recv()
        return self.at(*slot)

    def need_all(self):
        for chunk in range(len(self.messages)):
            for slot in SLOTS:
                self.need(slot, chunk)

    def own(self, chunk=0, sources=None):
        for i, (slot, to) in enumerate(self.messages[chunk]):
            if slot == (0, 0):
                self.step(i, chunk, sources and sources[to])

    def step(self, i, chunk=0, src=None):
        dst = self.slot(*self.need(self.messages[chunk][i][0], chunk), chunk)
        copy = self.copy(dst, dst if src is None else src, i, chunk)
        copy.start()
        self.pending.append(copy)


def kernel(
    h_ref, lists_ref, x_ref, f_ref, corr_ref, proj_ref,
    panels, lists, sib_list, index, halves, sib_half, packed, xs, ss, fs, rows, image,
    own_lists, part, parts,
    own_sem, panel_sems, list_sems, sib_list_sem, index_sem, half_sem, h_sems, h_sib_sems,
    x_sems, s_sems, f_sems, r_sems, r_sib_sems, part_sems, out_sem,
):
    r = lax.axis_index("row")
    c = lax.axis_index("col")
    k = lax.rem(r, 2)
    chip = r // 2
    y = lax.rem(chip, 4)
    zl = r // 8
    x = c // 2
    zh = lax.rem(c, 2)
    sibling = (r + 1 - 2 * k, c)
    pending = []

    def ring(v, d):
        return lax.rem(v + d + 4, 4)

    def row_device(z, yy):
        return (z * 8 + yy * 2 + k, c)

    def col_device(xx, z):
        return (r, xx * 2 + z)

    def remote(src, dst, sems, i, to, start=True):
        copy = pltpu.make_async_remote_copy(
            src_ref=src, dst_ref=dst, send_sem=sems.at[0, i], recv_sem=sems.at[1, i],
            device_id=to, device_id_type=MESH,
        )
        if start:
            copy.start()
            pending.append(copy)
        return copy

    row_peers = [((zl + dz) % 2, ring(y, dy)) for dz in (1, 0) for dy in (0, 1, 3, 2) if dz or dy]
    col_peers = [(ring(x, dx), (zh + dw) % 2) for dw in (1, 0) for dx in (2, 1, 3, 0) if dw or dx]

    own_panel = pltpu.make_async_copy(
        h_ref.at[:, :, pl.ds(pl.multiple_of((2 * y + zl) * 128, 128), 128)],
        panels.at[pl.ds(chip * 8, 8)], own_sem.at[0],
    )
    own_panel.start()
    x_src = x_ref.at[:, :, pl.ds(pl.multiple_of(r * 128, 128), 128)]
    own_x = pltpu.make_async_copy(x_src, xs.at[pl.ds(c * 16, 16)], own_sem.at[1])
    own_x.start()
    read_lists = pltpu.make_async_copy(lists_ref, own_lists, own_sem.at[2])
    read_lists.start()
    panels[64] = jnp.zeros((BLK, 128), jnp.bfloat16)

    barrier = pltpu.get_barrier_semaphore()
    for z, yy in row_peers:
        pl.semaphore_signal(barrier, inc=1, device_id=row_device(z, yy), device_id_type=MESH)
    for xx, z in col_peers:
        pl.semaphore_signal(barrier, inc=1, device_id=col_device(xx, z), device_id_type=MESH)
    across = (lax.rem(r + 8, 16), x * 2 + 1 - zh)
    for device in (sibling, across):
        pl.semaphore_signal(barrier, inc=1, device_id=device, device_id_type=MESH)
    read_lists.wait()
    lists[chip] = jnp.zeros((8, 128), jnp.int32)
    lists[chip, :, :K_NB] = own_lists[...]
    pl.semaphore_wait(barrier, 16)

    list_copies, panel_copies = [], []
    for i, (z, yy) in enumerate(row_peers):
        list_copies.append(remote(lists.at[chip], lists.at[chip], list_sems, i, row_device(z, yy)))
    def col_gather(buffer, sems, size, starts, pair, messages):
        def slot(p, w, t):
            return buffer.at[pl.ds((p * 2 + w) * 16 + starts[t], size)]

        devices = {"P": pair, "R": col_device(ring(x, 1), zh), "L": col_device(ring(x, -1), zh),
                   "X": col_device(ring(x, 2), zh)}
        return Gather(slot, x, zh, devices, sems, pending, messages)

    gx = col_gather(xs, x_sems, 8, (0, 8), across, (FORWARD,) * 2)
    x_across = x_ref.at[:, :, pl.ds(pl.multiple_of(lax.rem(r + 8, 16) * 128, 128), 128)]
    for t in range(2):
        half = pl.ds(8 * t, 8)
        gx.own(t, {"P": x_across.at[half], "R": x_src.at[half], "L": x_src.at[half]})

    for i, (z, yy) in enumerate(row_peers):
        src = h_ref.at[:, :, pl.ds(pl.multiple_of((2 * yy + z) * 128, 128), 128)]
        panel_copies.append(remote(src, panels.at[pl.ds(chip * 8, 8)], panel_sems, i, row_device(z, yy)))

    for copy in list_copies:
        copy.wait_recv()
    sib_lists = remote(lists.at[c], sib_list, sib_list_sem, 0, sibling)
    mine = pltpu.make_async_copy(lists.at[c], index.at[pl.ds(k * 8, 8)], index_sem.at[0])
    mine.start()
    sib_lists.wait_recv()
    theirs = pltpu.make_async_copy(sib_list, index.at[pl.ds((1 - k) * 8, 8)], index_sem.at[1])
    theirs.start()
    mine.wait()
    theirs.wait()

    pair_column = 4 * y + 2 * zl

    def pack_side(side):
        lane = lax.broadcasted_iota(jnp.int32, (BLK, 128), 1)
        line = lax.broadcasted_iota(jnp.int32, (BLK, 128), 0)
        blocks = []
        for s in range(K_NB):
            i = index[pair_column + side, s]
            blocks.append(panels[jnp.where(lax.rem(i // 8, 2) == k, 8 * (i // 16) + lax.rem(i, 8), 64)])
        pick = (lane == line + BLK * side).astype(jnp.bfloat16)
        return lax.dot_general(
            pick, jnp.concatenate(blocks, axis=0), (((1,), (1,)), ((), ())), preferred_element_type=jnp.float32
        ).astype(jnp.bfloat16)

    swaps = []

    def pack():
        own_panel.wait()
        for copy in panel_copies:
            copy.wait_recv()
        halves[0] = pack_side(1 - k)
        swaps.append(remote(halves.at[0], sib_half, half_sem, 0, sibling))
        halves[1] = pack_side(k)

    def add():
        swaps[0].wait_recv()
        packed[pair_column + k] = halves[1] + sib_half[...]

    def row_gather(slot, sems, messages):
        devices = {"P": row_device(1 - zl, y), "R": row_device(zl, ring(y, 1)), "L": row_device(zl, ring(y, -1)),
                   "X": row_device(zl, ring(y, 2))}
        return Gather(slot, y, zl, devices, sems, pending, messages)

    def h_slot(p, w, t):
        return packed.at[p * 4 + w * 2 + k, pl.ds(32 * t, 32)]

    gh = row_gather(h_slot, h_sems, (FORWARD,) * 2)
    h_sib = {}

    def pass_h(i, t):
        slot = h_slot(*gh.need(SLOTS[i], t), t)
        h_sib[i, t] = remote(slot, slot, h_sib_sems, 2 * i + t, sibling)

    def product(source, column):
        stacked = jnp.concatenate([source[index[column, s]] for s in range(K_NB)], axis=0)
        return jnp.dot(packed[column], stacked, preferred_element_type=jnp.float32)

    passes = (0, 1, 2, 3, 5, 4, 6, 7)
    starts = [4 * p + 2 * w for p, w in (gh.at(*SLOTS[i]) for i in passes)]
    across_z = col_device(x, 1 - zh)
    gs = col_gather(ss, s_sems, 2, starts, across_z, S_MESSAGES)

    def first_degree(u):
        if u == 0:
            own_x.wait()
            gx.need_all()
        for t in range(2):
            gh.need(SLOTS[passes[u]], t)
            h_sib[passes[u], t].wait_recv()
        for j in range(2):
            column = starts[u] + j
            at = c * 16 + column
            total = product(xs, column) - center_point * xs[at].astype(jnp.float32)
            ss[at] = (total / half_width).astype(jnp.bfloat16)
        gs.own(u)

    does = {"x": gx.step, "pack": pack, "add": add, "h": gh.step, "p": pass_h, "s": first_degree,
            "g": gs.step}
    for name, *args in FIRST:
        does[name](*args)
    gs.need_all()

    gf = col_gather(fs, f_sems, 4, (0, 4, 8, 12), across_z, F_MESSAGES)

    def r_slot(parity):
        def slot(p, w, t):
            return rows.at[w * 8 + p * 2 + parity, pl.ds(4 * t, 4)]

        return slot

    gr = row_gather(r_slot(k), r_sems, ROW_MESSAGES)
    r_sib = {}

    outs = []

    def write_out(group):
        copy = pltpu.make_async_copy(
            rows.at[group], f_ref.at[:, :, pl.ds(pl.multiple_of(group * 128, 128), 128)], out_sem.at[len(outs)]
        )
        copy.start()
        outs.append(copy)

    def pass_r(i):
        for t in range(4):
            p, w = gr.need(SLOTS[i], t)
        group = w * 8 + p * 2 + k
        r_sib[i] = remote(rows.at[group], rows.at[group], r_sib_sems, i, sibling)
        write_out(group)

    def second_degree(t):
        for j in range(4):
            column = t * 4 + j
            at = c * 16 + column
            total = product(ss, column) - center_point * ss[at].astype(jnp.float32)
            out = ((2.0 / half_width) * total - xs[at].astype(jnp.float32)).astype(jnp.bfloat16)
            fs[at] = out
            rows[r, column] = out
        gf.own(t)
        gr.own(t)

    does = {"f": second_degree, "a": gf.step, "r": gr.step, "q": pass_r}
    for name, *args in SECOND:
        does[name](*args)
    for i in range(8):
        p, w = gr.at(*SLOTS[i])
        r_sib[i].wait_recv()
        write_out(w * 8 + p * 2 + 1 - k)

    def project(which, left):
        def to(place, group):
            for half in range(2):
                place[:, half * 128:(half + 1) * 128] = lax.dot_general(
                    left, rows[group * 2 + half].reshape(1024, 128), (((0,), (0,)), ((), ())),
                    preferred_element_type=jnp.float32,
                ).astype(jnp.bfloat16)

        copies = []
        for i, (xx, z) in enumerate(col_peers):
            group = xx * 2 + z
            to(part.at[which, group], group)
            copies.append(
                remote(part.at[which, group], parts.at[which, c], part_sems, which * 7 + i, col_device(xx, z))
            )
        to(parts.at[which, c], c)
        return copies

    corr_copies = project(0, fs[pl.ds(c * 16, 16)].reshape(1024, 128))
    gf.need_all()

    @pl.loop(0, 4)
    def _(j):
        for i in range(4):
            column = j * 4 + i
            image[column] = product(fs, column).astype(jnp.bfloat16)

    proj_copies = project(1, image[...].reshape(1024, 128))

    for copy in pending[:-14]:
        copy.wait_send()
    for copy in outs:
        copy.wait()
    for copy in corr_copies:
        copy.wait_recv()
    corr_ref[...] = jnp.sum(parts[0].astype(jnp.float32), axis=0) / 8192.0
    for copy in proj_copies:
        copy.wait_recv()
    proj_ref[...] = jnp.sum(parts[1].astype(jnp.float32), axis=0) / 8192.0
    for copy in corr_copies + proj_copies:
        copy.wait_send()


def shards(hamiltonian, block_cols, start_vectors):
    bf16, f32, dma = jnp.bfloat16, jnp.float32, pltpu.SemaphoreType.DMA
    vmem = pltpu.VMEM
    place = pl.BlockSpec(memory_space=pl.ANY)
    out_shape = (
        jax.ShapeDtypeStruct((16, BLK, 2048), bf16),
        jax.ShapeDtypeStruct((128, 256), f32),
        jax.ShapeDtypeStruct((128, 256), f32),
    )
    results = pl.pallas_call(
        kernel,
        out_shape=out_shape,
        in_specs=[place] * 3,
        out_specs=(place, pl.BlockSpec(memory_space=pltpu.VMEM), pl.BlockSpec(memory_space=pltpu.VMEM)),
        scratch_shapes=[
            vmem((65, BLK, 128), bf16),
            vmem((8, 8, 128), jnp.int32),
            vmem((8, 128), jnp.int32),
            pltpu.SMEM((16, 128), jnp.int32),
            vmem((2, BLK, DEPTH), bf16),
            vmem((BLK, DEPTH), bf16),
            vmem((16, BLK, DEPTH), bf16),
            vmem((128, BLK, 128), bf16),
            vmem((128, BLK, 128), bf16),
            vmem((128, BLK, 128), bf16),
            vmem((16, 16, BLK, 128), bf16),
            vmem((16, BLK, 128), bf16),
            vmem((8, K_NB), jnp.int32),
            vmem((2, 8, 128, 256), bf16),
            vmem((2, 8, 128, 256), bf16),
            dma((3,)),
            dma((2, 7)),
            dma((2, 7)),
            dma((2, 1)),
            dma((2,)),
            dma((2, 1)),
            dma((2, 7, 2)),
            dma((2, 16)),
            dma((2, 7, 2)),
            dma((2, 7, 8)),
            dma((2, 7, 4)),
            dma((2, 7, 4)),
            dma((2, 8)),
            dma((2, 14)),
            dma((16,)),
        ],
        compiler_params=pltpu.CompilerParams(
            collective_id=0, has_side_effects=True, vmem_limit_bytes=48 * 1024 * 1024
        ),
    )(hamiltonian.reshape(8, BLK, 1024), block_cols, start_vectors.reshape(16, BLK, 2048))

    def hand_on(*refs):
        copies = [pltpu.make_async_copy(refs[i], refs[3 + i], refs[6].at[i]) for i in (1, 2)]
        for i in range(4):
            part = pl.ds(4 * i, 4)
            copies.append(pltpu.make_async_copy(refs[0].at[part], refs[3].at[part], refs[6].at[3 + i]))
        for copy in copies:
            copy.start()
        for copy in copies:
            copy.wait()

    f, corr, proj = pl.pallas_call(
        hand_on,
        out_shape=out_shape,
        in_specs=[place] * 3,
        out_specs=(place,) * 3,
        scratch_shapes=[dma((7,))],
        compiler_params=pltpu.CompilerParams(vmem_limit_bytes=40 * 1024 * 1024),
    )(*results)
    return f.reshape(1024, 2048), corr, proj


def solution(mesh):
    in_specs = (P("row", "col"), P("row", None), P("col", None))
    out_specs = (P("col", None), P("row", "col"), P("row", "col"))
    return jax.shard_map(shards, mesh=mesh, in_specs=in_specs, out_specs=out_specs, check_vma=False)
```

```python
import jax
import jax.numpy as jnp
from jax import lax
from jax.experimental import pallas as pl
from jax.experimental.pallas import tpu as pltpu
from jax.sharding import PartitionSpec as P

BLK = 64
K_NB = 26
DEPTH = K_NB * BLK
MESH = pl.DeviceIdType.MESH
center_point = 0.2
half_width = 0.8

FORWARD = (((0, 0), "P"), ((0, 0), "R"), ((0, 0), "L"), ((0, 1), "R"),
           ((0, 1), "L"), ((-1, 0), "R"), ((1, 1), "L"))
PAIR_LAST_RIGHT = (((0, 0), "P"), ((0, 0), "R"), ((0, 0), "L"), ((-1, 0), "P"),
                   ((1, 0), "P"), ((-1, 0), "R"), ((2, 0), "P"))
PAIR_LAST_LEFT = (((0, 0), "P"), ((0, 0), "R"), ((0, 0), "L"), ((-1, 0), "P"),
                  ((1, 0), "P"), ((1, 0), "L"), ((2, 0), "P"))
PAIR_LAST_DIRECT = (((0, 0), "P"), ((0, 0), "R"), ((0, 0), "L"), ((-1, 0), "P"),
                    ((1, 0), "P"), ((0, 0), "X"), ((2, 0), "P"))
DIRECT = (((0, 0), "P"), ((0, 0), "R"), ((0, 0), "L"), ((0, 1), "R"),
          ((0, 1), "L"), ((0, 0), "X"), ((0, 1), "X"))
S_MESSAGES = (DIRECT, PAIR_LAST_LEFT, PAIR_LAST_LEFT, FORWARD, PAIR_LAST_RIGHT, FORWARD, PAIR_LAST_DIRECT, DIRECT)
F_MESSAGES = (FORWARD, FORWARD, FORWARD, FORWARD)
ROW_MESSAGES = (FORWARD, FORWARD, FORWARD, FORWARD)
SLOTS = ((0, 0), (0, 1), (-1, 0), (1, 0), (-1, 1), (1, 1), (2, 0), (2, 1))
FIRST = (
    ("x", 5, 0), ("x", 3, 0), ("x", 4, 0), ("x", 5, 1), ("x", 3, 1), ("x", 4, 1), ("pack",), ("x", 6, 0), ("add",),
    ("h", 0, 0), ("h", 1, 0), ("h", 2, 0), ("p", 0, 0), ("h", 0, 1), ("h", 1, 1), ("h", 2, 1), ("p", 0, 1),
    ("x", 6, 1), ("h", 3, 0), ("h", 4, 0), ("p", 1, 0), ("h", 5, 0), ("p", 2, 0), ("p", 3, 0), ("h", 3, 1),
    ("h", 4, 1), ("p", 1, 1), ("h", 5, 1), ("p", 2, 1), ("p", 3, 1), ("s", 0), ("s", 1), ("g", 3, 0), ("g", 4, 0),
    ("p", 4, 0), ("h", 6, 0), ("p", 5, 0), ("g", 6, 0), ("s", 2), ("s", 3), ("g", 3, 1), ("g", 4, 1), ("p", 6, 0),
    ("h", 6, 1), ("p", 5, 1), ("g", 5, 1), ("s", 4), ("g", 3, 2), ("p", 4, 1), ("p", 7, 0), ("g", 4, 2), ("g", 5, 2),
    ("g", 3, 3), ("g", 4, 3), ("g", 5, 3), ("g", 6, 1), ("s", 5), ("p", 6, 1), ("g", 3, 4), ("p", 7, 1), ("g", 5, 4),
    ("g", 4, 4), ("g", 6, 2), ("s", 6), ("g", 6, 3), ("s", 7), ("g", 5, 5), ("g", 6, 4), ("g", 3, 5), ("g", 4, 5),
    ("g", 3, 6), ("g", 4, 6), ("g", 6, 6), ("g", 3, 7), ("g", 4, 7), ("g", 6, 7), ("g", 6, 5),
)
SECOND = (
    ("f", 0), ("f", 1), ("f", 2), ("f", 3), ("q", 0), ("r", 5, 0), ("r", 3, 0), ("r", 4, 0), ("a", 5, 0), ("a", 3, 0),
    ("a", 4, 0), ("r", 5, 1), ("r", 3, 1), ("r", 4, 1), ("a", 5, 1), ("a", 3, 1), ("a", 4, 1), ("r", 5, 2),
    ("r", 3, 2), ("r", 4, 2), ("a", 5, 2), ("a", 3, 2), ("a", 4, 2), ("r", 5, 3), ("r", 3, 3), ("r", 4, 3),
    ("a", 5, 3), ("a", 3, 3), ("a", 4, 3), ("q", 1), ("q", 2), ("q", 3), ("r", 6, 0), ("a", 6, 0), ("r", 6, 1),
    ("a", 6, 1), ("r", 6, 2), ("a", 6, 2), ("r", 6, 3), ("a", 6, 3), ("q", 5), ("q", 4), ("q", 6), ("q", 7),
)


def same(slot):
    return slot[0] % 4, slot[1] % 2


def comes(message):
    (dp, dw), to = message
    return same({"P": (dp, dw + 1), "R": (dp - 1, dw), "L": (dp + 1, dw), "X": (dp + 2, dw)}[to])


class Gather:
    def __init__(self, slot, p, w, devices, sems, pending, messages):
        self.slot, self.p, self.w, self.devices = slot, p, w, devices
        self.send_sem, self.recv_sem, self.pending = sems.at[0], sems.at[1], pending
        self.messages = messages
        self.waited = set()

    def at(self, dp, dw):
        return lax.rem(self.p + dp + 4, 4), (self.w + dw) % 2

    def copy(self, ref, src, i, chunk):
        return pltpu.make_async_remote_copy(
            src_ref=src,
            dst_ref=ref,
            send_sem=self.send_sem.at[i, chunk],
            recv_sem=self.recv_sem.at[i, chunk],
            device_id=self.devices[self.messages[chunk][i][1]],
            device_id_type=MESH,
        )

    def carrier(self, slot, chunk):
        brings = [comes(message) for message in self.messages[chunk]]
        return None if same(slot) == (0, 0) else brings.index(same(slot))

    def need(self, slot, chunk=0):
        i = self.carrier(slot, chunk)
        if i is not None and (i, chunk) not in self.waited:
            self.waited.add((i, chunk))
            ref = self.slot(*self.at(*slot), chunk)
            self.copy(ref, ref, i, chunk).wait_recv()
        return self.at(*slot)

    def need_all(self):
        for chunk in range(len(self.messages)):
            for slot in SLOTS:
                self.need(slot, chunk)

    def own(self, chunk=0, sources=None):
        for i, (slot, to) in enumerate(self.messages[chunk]):
            if slot == (0, 0):
                self.step(i, chunk, sources and sources[to])

    def step(self, i, chunk=0, src=None):
        dst = self.slot(*self.need(self.messages[chunk][i][0], chunk), chunk)
        copy = self.copy(dst, dst if src is None else src, i, chunk)
        copy.start()
        self.pending.append(copy)


def kernel(
    h_ref, lists_ref, x_ref, f_ref, corr_ref, proj_ref,
    panels, lists, sib_list, index, halves, sib_half, packed, xs, ss, fs, rows, image,
    own_lists, part, parts,
    own_sem, panel_sems, list_sems, sib_list_sem, index_sem, half_sem, h_sems, h_sib_sems,
    x_sems, s_sems, f_sems, r_sems, r_sib_sems, part_sems, out_sem,
):
    r = lax.axis_index("row")
    c = lax.axis_index("col")
    k = lax.rem(r, 2)
    chip = r // 2
    y = lax.rem(chip, 4)
    zl = r // 8
    x = c // 2
    zh = lax.rem(c, 2)
    sibling = (r + 1 - 2 * k, c)
    pending = []

    def ring(v, d):
        return lax.rem(v + d + 4, 4)

    def row_device(z, yy):
        return (z * 8 + yy * 2 + k, c)

    def col_device(xx, z):
        return (r, xx * 2 + z)

    def remote(src, dst, sems, i, to, start=True):
        copy = pltpu.make_async_remote_copy(
            src_ref=src, dst_ref=dst, send_sem=sems.at[0, i], recv_sem=sems.at[1, i],
            device_id=to, device_id_type=MESH,
        )
        if start:
            copy.start()
            pending.append(copy)
        return copy

    row_peers = [((zl + dz) % 2, ring(y, dy)) for dz in (1, 0) for dy in (0, 1, 3, 2) if dz or dy]
    col_peers = [(ring(x, dx), (zh + dw) % 2) for dw in (1, 0) for dx in (2, 1, 3, 0) if dw or dx]

    own_panel = pltpu.make_async_copy(
        h_ref.at[:, :, pl.ds(pl.multiple_of((2 * y + zl) * 128, 128), 128)],
        panels.at[pl.ds(chip * 8, 8)], own_sem.at[0],
    )
    own_panel.start()
    x_src = x_ref.at[:, :, pl.ds(pl.multiple_of(r * 128, 128), 128)]
    own_x = pltpu.make_async_copy(x_src, xs.at[pl.ds(c * 16, 16)], own_sem.at[1])
    own_x.start()
    read_lists = pltpu.make_async_copy(lists_ref, own_lists, own_sem.at[2])
    read_lists.start()
    panels[64] = jnp.zeros((BLK, 128), jnp.bfloat16)

    barrier = pltpu.get_barrier_semaphore()
    for z, yy in row_peers:
        pl.semaphore_signal(barrier, inc=1, device_id=row_device(z, yy), device_id_type=MESH)
    for xx, z in ((ring(x, 1), zh), (ring(x, -1), zh), (x, 1 - zh), (ring(x, 2), zh)):
        pl.semaphore_signal(barrier, inc=1, device_id=col_device(xx, z), device_id_type=MESH)
    across = (lax.rem(r + 8, 16), x * 2 + 1 - zh)
    for device in (sibling, across):
        pl.semaphore_signal(barrier, inc=1, device_id=device, device_id_type=MESH)
    read_lists.wait()
    lists[chip] = jnp.zeros((8, 128), jnp.int32)
    lists[chip, :, :K_NB] = own_lists[...]
    pl.semaphore_wait(barrier, 13)

    list_copies, panel_copies = [], []
    for i, (z, yy) in enumerate(row_peers):
        list_copies.append(remote(lists.at[chip], lists.at[chip], list_sems, i, row_device(z, yy)))
    def col_gather(buffer, sems, size, starts, pair, messages):
        def slot(p, w, t):
            return buffer.at[pl.ds((p * 2 + w) * 16 + starts[t], size)]

        devices = {"P": pair, "R": col_device(ring(x, 1), zh), "L": col_device(ring(x, -1), zh),
                   "X": col_device(ring(x, 2), zh)}
        return Gather(slot, x, zh, devices, sems, pending, messages)

    gx = col_gather(xs, x_sems, 8, (0, 8), across, (FORWARD,) * 2)
    x_across = x_ref.at[:, :, pl.ds(pl.multiple_of(lax.rem(r + 8, 16) * 128, 128), 128)]
    for t in range(2):
        half = pl.ds(8 * t, 8)
        gx.own(t, {"P": x_across.at[half], "R": x_src.at[half], "L": x_src.at[half]})

    for i, (z, yy) in enumerate(row_peers):
        src = h_ref.at[:, :, pl.ds(pl.multiple_of((2 * yy + z) * 128, 128), 128)]
        panel_copies.append(remote(src, panels.at[pl.ds(chip * 8, 8)], panel_sems, i, row_device(z, yy)))

    for copy in list_copies:
        copy.wait_recv()
    sib_lists = remote(lists.at[c], sib_list, sib_list_sem, 0, sibling)
    mine = pltpu.make_async_copy(lists.at[c], index.at[pl.ds(k * 8, 8)], index_sem.at[0])
    mine.start()
    sib_lists.wait_recv()
    theirs = pltpu.make_async_copy(sib_list, index.at[pl.ds((1 - k) * 8, 8)], index_sem.at[1])
    theirs.start()
    mine.wait()
    theirs.wait()

    pair_column = 4 * y + 2 * zl

    def pack_side(side):
        lane = lax.broadcasted_iota(jnp.int32, (BLK, 128), 1)
        line = lax.broadcasted_iota(jnp.int32, (BLK, 128), 0)
        blocks = []
        for s in range(K_NB):
            i = index[pair_column + side, s]
            blocks.append(panels[jnp.where(lax.rem(i // 8, 2) == k, 8 * (i // 16) + lax.rem(i, 8), 64)])
        pick = (lane == line + BLK * side).astype(jnp.bfloat16)
        return lax.dot_general(
            pick, jnp.concatenate(blocks, axis=0), (((1,), (1,)), ((), ())), preferred_element_type=jnp.float32
        ).astype(jnp.bfloat16)

    swaps = []

    def pack():
        own_panel.wait()
        for copy in panel_copies:
            copy.wait_recv()
        halves[0] = pack_side(1 - k)
        swaps.append(remote(halves.at[0], sib_half, half_sem, 0, sibling))
        halves[1] = pack_side(k)

    def add():
        swaps[0].wait_recv()
        packed[pair_column + k] = halves[1] + sib_half[...]

    def row_gather(slot, sems, messages):
        devices = {"P": row_device(1 - zl, y), "R": row_device(zl, ring(y, 1)), "L": row_device(zl, ring(y, -1)),
                   "X": row_device(zl, ring(y, 2))}
        return Gather(slot, y, zl, devices, sems, pending, messages)

    def h_slot(p, w, t):
        return packed.at[p * 4 + w * 2 + k, pl.ds(32 * t, 32)]

    gh = row_gather(h_slot, h_sems, (FORWARD,) * 2)
    h_sib = {}

    def pass_h(i, t):
        slot = h_slot(*gh.need(SLOTS[i], t), t)
        h_sib[i, t] = remote(slot, slot, h_sib_sems, 2 * i + t, sibling)

    def product(source, column):
        stacked = jnp.concatenate([source[index[column, s]] for s in range(K_NB)], axis=0)
        return jnp.dot(packed[column], stacked, preferred_element_type=jnp.float32)

    passes = (0, 1, 2, 3, 5, 4, 6, 7)
    starts = [4 * p + 2 * w for p, w in (gh.at(*SLOTS[i]) for i in passes)]
    across_z = col_device(x, 1 - zh)
    gs = col_gather(ss, s_sems, 2, starts, across_z, S_MESSAGES)

    def first_degree(u):
        if u == 0:
            own_x.wait()
            gx.need_all()
        for t in range(2):
            gh.need(SLOTS[passes[u]], t)
            h_sib[passes[u], t].wait_recv()
        for j in range(2):
            column = starts[u] + j
            at = c * 16 + column
            total = product(xs, column) - center_point * xs[at].astype(jnp.float32)
            ss[at] = (total / half_width).astype(jnp.bfloat16)
        gs.own(u)

    does = {"x": gx.step, "pack": pack, "add": add, "h": gh.step, "p": pass_h, "s": first_degree,
            "g": gs.step}
    for name, *args in FIRST:
        does[name](*args)
    gs.need_all()

    gf = col_gather(fs, f_sems, 4, (0, 4, 8, 12), across_z, F_MESSAGES)

    def r_slot(parity):
        def slot(p, w, t):
            return rows.at[w * 8 + p * 2 + parity, pl.ds(4 * t, 4)]

        return slot

    gr = row_gather(r_slot(k), r_sems, ROW_MESSAGES)
    r_sib = {}

    outs = []

    def write_out(group):
        copy = pltpu.make_async_copy(
            rows.at[group], f_ref.at[:, :, pl.ds(pl.multiple_of(group * 128, 128), 128)], out_sem.at[len(outs)]
        )
        copy.start()
        outs.append(copy)

    def pass_r(i):
        for t in range(4):
            p, w = gr.need(SLOTS[i], t)
        group = w * 8 + p * 2 + k
        r_sib[i] = remote(rows.at[group], rows.at[group], r_sib_sems, i, sibling)
        write_out(group)

    def second_degree(t):
        for j in range(4):
            column = t * 4 + j
            at = c * 16 + column
            total = product(ss, column) - center_point * ss[at].astype(jnp.float32)
            out = ((2.0 / half_width) * total - xs[at].astype(jnp.float32)).astype(jnp.bfloat16)
            fs[at] = out
            rows[r, column] = out
        gf.own(t)
        gr.own(t)

    does = {"f": second_degree, "a": gf.step, "r": gr.step, "q": pass_r}
    for name, *args in SECOND:
        does[name](*args)
    for i in range(8):
        p, w = gr.at(*SLOTS[i])
        r_sib[i].wait_recv()
        write_out(w * 8 + p * 2 + 1 - k)

    def project(which, left):
        def to(place, group):
            for half in range(2):
                place[:, half * 128:(half + 1) * 128] = lax.dot_general(
                    left, rows[group * 2 + half].reshape(1024, 128), (((0,), (0,)), ((), ())),
                    preferred_element_type=jnp.float32,
                ).astype(jnp.bfloat16)

        copies = []
        for i, (xx, z) in enumerate(col_peers):
            group = xx * 2 + z
            to(part.at[which, group], group)
            copies.append(
                remote(part.at[which, group], parts.at[which, c], part_sems, which * 7 + i, col_device(xx, z))
            )
        to(parts.at[which, c], c)
        return copies

    corr_copies = project(0, fs[pl.ds(c * 16, 16)].reshape(1024, 128))
    gf.need_all()

    @pl.loop(0, 4)
    def _(j):
        for i in range(4):
            column = j * 4 + i
            image[column] = product(fs, column).astype(jnp.bfloat16)

    proj_copies = project(1, image[...].reshape(1024, 128))

    for copy in pending[:-14]:
        copy.wait_send()
    for copy in outs:
        copy.wait()
    for copy in corr_copies:
        copy.wait_recv()
    corr_ref[...] = jnp.sum(parts[0].astype(jnp.float32), axis=0) / 8192.0
    for copy in proj_copies:
        copy.wait_recv()
    proj_ref[...] = jnp.sum(parts[1].astype(jnp.float32), axis=0) / 8192.0
    for copy in corr_copies + proj_copies:
        copy.wait_send()


def shards(hamiltonian, block_cols, start_vectors):
    bf16, f32, dma = jnp.bfloat16, jnp.float32, pltpu.SemaphoreType.DMA
    vmem = pltpu.VMEM
    place = pl.BlockSpec(memory_space=pl.ANY)
    out_shape = (
        jax.ShapeDtypeStruct((16, BLK, 2048), bf16),
        jax.ShapeDtypeStruct((128, 256), f32),
        jax.ShapeDtypeStruct((128, 256), f32),
    )
    results = pl.pallas_call(
        kernel,
        out_shape=out_shape,
        in_specs=[place] * 3,
        out_specs=(place, pl.BlockSpec(memory_space=pltpu.VMEM), pl.BlockSpec(memory_space=pltpu.VMEM)),
        scratch_shapes=[
            vmem((65, BLK, 128), bf16),
            vmem((8, 8, 128), jnp.int32),
            vmem((8, 128), jnp.int32),
            pltpu.SMEM((16, 128), jnp.int32),
            vmem((2, BLK, DEPTH), bf16),
            vmem((BLK, DEPTH), bf16),
            vmem((16, BLK, DEPTH), bf16),
            vmem((128, BLK, 128), bf16),
            vmem((128, BLK, 128), bf16),
            vmem((128, BLK, 128), bf16),
            vmem((16, 16, BLK, 128), bf16),
            vmem((16, BLK, 128), bf16),
            vmem((8, K_NB), jnp.int32),
            vmem((2, 8, 128, 256), bf16),
            vmem((2, 8, 128, 256), bf16),
            dma((3,)),
            dma((2, 7)),
            dma((2, 7)),
            dma((2, 1)),
            dma((2,)),
            dma((2, 1)),
            dma((2, 7, 2)),
            dma((2, 16)),
            dma((2, 7, 2)),
            dma((2, 7, 8)),
            dma((2, 7, 4)),
            dma((2, 7, 4)),
            dma((2, 8)),
            dma((2, 14)),
            dma((16,)),
        ],
        compiler_params=pltpu.CompilerParams(
            collective_id=0, has_side_effects=True, vmem_limit_bytes=48 * 1024 * 1024
        ),
    )(hamiltonian.reshape(8, BLK, 1024), block_cols, start_vectors.reshape(16, BLK, 2048))

    def hand_on(*refs):
        copies = [pltpu.make_async_copy(refs[i], refs[3 + i], refs[6].at[i]) for i in (1, 2)]
        for i in range(4):
            part = pl.ds(4 * i, 4)
            copies.append(pltpu.make_async_copy(refs[0].at[part], refs[3].at[part], refs[6].at[3 + i]))
        for copy in copies:
            copy.start()
        for copy in copies:
            copy.wait()

    f, corr, proj = pl.pallas_call(
        hand_on,
        out_shape=out_shape,
        in_specs=[place] * 3,
        out_specs=(place,) * 3,
        scratch_shapes=[dma((7,))],
        compiler_params=pltpu.CompilerParams(vmem_limit_bytes=40 * 1024 * 1024),
    )(*results)
    return f.reshape(1024, 2048), corr, proj


def solution(mesh):
    in_specs = (P("row", "col"), P("row", None), P("col", None))
    out_specs = (P("col", None), P("row", "col"), P("row", "col"))
    return jax.shard_map(shards, mesh=mesh, in_specs=in_specs, out_specs=out_specs, check_vma=False)
```

```python
import jax
import jax.numpy as jnp
from jax import lax
from jax.experimental import pallas as pl
from jax.experimental.pallas import tpu as pltpu
from jax.sharding import PartitionSpec as P

BLK = 64
K_NB = 26
DEPTH = K_NB * BLK
MESH = pl.DeviceIdType.MESH
center_point = 0.2
half_width = 0.8

FORWARD = (((0, 0), "P"), ((0, 0), "R"), ((0, 0), "L"), ((0, 1), "R"),
           ((0, 1), "L"), ((-1, 0), "R"), ((1, 1), "L"))
PAIR_LAST_RIGHT = (((0, 0), "P"), ((0, 0), "R"), ((0, 0), "L"), ((-1, 0), "P"),
                   ((1, 0), "P"), ((-1, 0), "R"), ((2, 0), "P"))
PAIR_LAST_LEFT = (((0, 0), "P"), ((0, 0), "R"), ((0, 0), "L"), ((-1, 0), "P"),
                  ((1, 0), "P"), ((1, 0), "L"), ((2, 0), "P"))
PAIR_LAST_DIRECT = (((0, 0), "P"), ((0, 0), "R"), ((0, 0), "L"), ((-1, 0), "P"),
                    ((1, 0), "P"), ((0, 0), "X"), ((2, 0), "P"))
DIRECT = (((0, 0), "P"), ((0, 0), "R"), ((0, 0), "L"), ((0, 1), "R"),
          ((0, 1), "L"), ((0, 0), "X"), ((0, 1), "X"))
S_MESSAGES = (DIRECT, PAIR_LAST_LEFT, PAIR_LAST_LEFT, FORWARD, PAIR_LAST_RIGHT, FORWARD, PAIR_LAST_DIRECT, DIRECT)
F_MESSAGES = (FORWARD, FORWARD, FORWARD, FORWARD)
ROW_MESSAGES = (FORWARD, FORWARD, FORWARD, FORWARD)
SLOTS = ((0, 0), (0, 1), (-1, 0), (1, 0), (-1, 1), (1, 1), (2, 0), (2, 1))
FIRST = (
    ("x", 5, 0), ("x", 3, 0), ("x", 4, 0), ("x", 5, 1), ("x", 3, 1), ("x", 4, 1), ("pack",), ("x", 6, 0), ("add",),
    ("h", 0, 0), ("h", 1, 0), ("h", 2, 0), ("p", 0, 0), ("h", 0, 1), ("h", 1, 1), ("h", 2, 1), ("p", 0, 1),
    ("x", 6, 1), ("h", 3, 0), ("h", 4, 0), ("p", 1, 0), ("h", 5, 0), ("p", 2, 0), ("p", 3, 0), ("h", 3, 1),
    ("h", 4, 1), ("p", 1, 1), ("h", 5, 1), ("p", 2, 1), ("p", 3, 1), ("s", 0), ("s", 1), ("g", 3, 0), ("g", 4, 0),
    ("p", 4, 0), ("h", 6, 0), ("p", 5, 0), ("g", 6, 0), ("s", 2), ("s", 3), ("g", 3, 1), ("g", 4, 1), ("p", 6, 0),
    ("h", 6, 1), ("p", 5, 1), ("g", 5, 1), ("s", 4), ("g", 3, 2), ("p", 4, 1), ("p", 7, 0), ("g", 4, 2), ("g", 5, 2),
    ("g", 3, 3), ("g", 4, 3), ("g", 5, 3), ("g", 6, 1), ("s", 5), ("p", 6, 1), ("g", 3, 4), ("p", 7, 1), ("g", 5, 4),
    ("g", 4, 4), ("g", 6, 2), ("s", 6), ("g", 6, 3), ("s", 7), ("g", 5, 5), ("g", 6, 4), ("g", 3, 5), ("g", 4, 5),
    ("g", 3, 6), ("g", 4, 6), ("g", 6, 6), ("g", 3, 7), ("g", 4, 7), ("g", 6, 7), ("g", 6, 5),
)
SECOND = (
    ("f", 0), ("f", 1), ("f", 2), ("f", 3), ("q", 0), ("r", 5, 0), ("r", 3, 0), ("r", 4, 0), ("a", 5, 0), ("a", 3, 0),
    ("a", 4, 0), ("r", 5, 1), ("r", 3, 1), ("r", 4, 1), ("a", 5, 1), ("a", 3, 1), ("a", 4, 1), ("r", 5, 2),
    ("r", 3, 2), ("r", 4, 2), ("a", 5, 2), ("a", 3, 2), ("a", 4, 2), ("r", 5, 3), ("r", 3, 3), ("r", 4, 3),
    ("a", 5, 3), ("a", 3, 3), ("a", 4, 3), ("q", 1), ("q", 2), ("q", 3), ("r", 6, 0), ("a", 6, 0), ("r", 6, 1),
    ("a", 6, 1), ("r", 6, 2), ("a", 6, 2), ("r", 6, 3), ("a", 6, 3), ("q", 5), ("q", 4), ("q", 6), ("q", 7),
)


def same(slot):
    return slot[0] % 4, slot[1] % 2


def comes(message):
    (dp, dw), to = message
    return same({"P": (dp, dw + 1), "R": (dp - 1, dw), "L": (dp + 1, dw), "X": (dp + 2, dw)}[to])


class Gather:
    def __init__(self, slot, p, w, devices, sems, pending, messages):
        self.slot, self.p, self.w, self.devices = slot, p, w, devices
        self.send_sem, self.recv_sem, self.pending = sems.at[0], sems.at[1], pending
        self.messages = messages
        self.waited = set()

    def at(self, dp, dw):
        return lax.rem(self.p + dp + 4, 4), (self.w + dw) % 2

    def copy(self, ref, src, i, chunk):
        return pltpu.make_async_remote_copy(
            src_ref=src,
            dst_ref=ref,
            send_sem=self.send_sem.at[i, chunk],
            recv_sem=self.recv_sem.at[i, chunk],
            device_id=self.devices[self.messages[chunk][i][1]],
            device_id_type=MESH,
        )

    def carrier(self, slot, chunk):
        brings = [comes(message) for message in self.messages[chunk]]
        return None if same(slot) == (0, 0) else brings.index(same(slot))

    def need(self, slot, chunk=0):
        i = self.carrier(slot, chunk)
        if i is not None and (i, chunk) not in self.waited:
            self.waited.add((i, chunk))
            ref = self.slot(*self.at(*slot), chunk)
            self.copy(ref, ref, i, chunk).wait_recv()
        return self.at(*slot)

    def need_all(self):
        for chunk in range(len(self.messages)):
            for slot in SLOTS:
                self.need(slot, chunk)

    def own(self, chunk=0, sources=None):
        for i, (slot, to) in enumerate(self.messages[chunk]):
            if slot == (0, 0):
                self.step(i, chunk, sources and sources[to])

    def step(self, i, chunk=0, src=None):
        dst = self.slot(*self.need(self.messages[chunk][i][0], chunk), chunk)
        copy = self.copy(dst, dst if src is None else src, i, chunk)
        copy.start()
        self.pending.append(copy)


def kernel(
    h_ref, lists_ref, x_ref, f_ref, corr_ref, proj_ref,
    panels, lists, sib_list, index, halves, sib_half, packed, xs, ss, fs, rows, image,
    own_lists, part, parts,
    own_sem, panel_sems, list_sems, sib_list_sem, index_sem, half_sem, h_sems, h_sib_sems,
    x_sems, s_sems, f_sems, r_sems, r_sib_sems, part_sems, out_sem,
):
    r = lax.axis_index("row")
    c = lax.axis_index("col")
    k = lax.rem(r, 2)
    chip = r // 2
    y = lax.rem(chip, 4)
    zl = r // 8
    x = c // 2
    zh = lax.rem(c, 2)
    sibling = (r + 1 - 2 * k, c)
    pending = []

    def ring(v, d):
        return lax.rem(v + d + 4, 4)

    def row_device(z, yy):
        return (z * 8 + yy * 2 + k, c)

    def col_device(xx, z):
        return (r, xx * 2 + z)

    def remote(src, dst, sems, i, to, start=True):
        copy = pltpu.make_async_remote_copy(
            src_ref=src, dst_ref=dst, send_sem=sems.at[0, i], recv_sem=sems.at[1, i],
            device_id=to, device_id_type=MESH,
        )
        if start:
            copy.start()
            pending.append(copy)
        return copy

    row_peers = [((zl + dz) % 2, ring(y, dy)) for dz in (1, 0) for dy in (0, 1, 3, 2) if dz or dy]
    col_peers = [(ring(x, dx), (zh + dw) % 2) for dw in (1, 0) for dx in (2, 1, 3, 0) if dw or dx]

    own_panel = pltpu.make_async_copy(
        h_ref.at[:, :, pl.ds(pl.multiple_of((2 * y + zl) * 128, 128), 128)],
        panels.at[pl.ds(chip * 8, 8)], own_sem.at[0],
    )
    own_panel.start()
    x_src = x_ref.at[:, :, pl.ds(pl.multiple_of(r * 128, 128), 128)]
    own_x = pltpu.make_async_copy(x_src, xs.at[pl.ds(c * 16, 16)], own_sem.at[1])
    own_x.start()
    read_lists = pltpu.make_async_copy(lists_ref, own_lists, own_sem.at[2])
    read_lists.start()
    panels[64] = jnp.zeros((BLK, 128), jnp.bfloat16)

    barrier = pltpu.get_barrier_semaphore()
    for z, yy in row_peers:
        pl.semaphore_signal(barrier, inc=1, device_id=row_device(z, yy), device_id_type=MESH)
    for xx, z in ((ring(x, 1), zh), (ring(x, -1), zh), (x, 1 - zh), (ring(x, 2), zh)):
        pl.semaphore_signal(barrier, inc=1, device_id=col_device(xx, z), device_id_type=MESH)
    across = (lax.rem(r + 8, 16), x * 2 + 1 - zh)
    for device in (sibling, across):
        pl.semaphore_signal(barrier, inc=1, device_id=device, device_id_type=MESH)
    read_lists.wait()
    lists[chip] = jnp.zeros((8, 128), jnp.int32)
    lists[chip, :, :K_NB] = own_lists[...]
    pl.semaphore_wait(barrier, 13)

    list_copies, panel_copies = [], []
    for i, (z, yy) in enumerate(row_peers):
        list_copies.append(remote(lists.at[chip], lists.at[chip], list_sems, i, row_device(z, yy)))
    def col_gather(buffer, sems, size, starts, pair, messages):
        def slot(p, w, t):
            return buffer.at[pl.ds((p * 2 + w) * 16 + starts[t], size)]

        devices = {"P": pair, "R": col_device(ring(x, 1), zh), "L": col_device(ring(x, -1), zh),
                   "X": col_device(ring(x, 2), zh)}
        return Gather(slot, x, zh, devices, sems, pending, messages)

    gx = col_gather(xs, x_sems, 8, (0, 8), across, (FORWARD,) * 2)
    x_across = x_ref.at[:, :, pl.ds(pl.multiple_of(lax.rem(r + 8, 16) * 128, 128), 128)]
    for t in range(2):
        half = pl.ds(8 * t, 8)
        gx.own(t, {"P": x_across.at[half], "R": x_src.at[half], "L": x_src.at[half]})

    for i, (z, yy) in enumerate(row_peers):
        src = h_ref.at[:, :, pl.ds(pl.multiple_of((2 * yy + z) * 128, 128), 128)]
        panel_copies.append(remote(src, panels.at[pl.ds(chip * 8, 8)], panel_sems, i, row_device(z, yy)))

    for copy in list_copies:
        copy.wait_recv()
    sib_lists = remote(lists.at[c], sib_list, sib_list_sem, 0, sibling)
    mine = pltpu.make_async_copy(lists.at[c], index.at[pl.ds(k * 8, 8)], index_sem.at[0])
    mine.start()
    sib_lists.wait_recv()
    theirs = pltpu.make_async_copy(sib_list, index.at[pl.ds((1 - k) * 8, 8)], index_sem.at[1])
    theirs.start()
    mine.wait()
    theirs.wait()

    pair_column = 4 * y + 2 * zl

    def pack_side(side):
        lane = lax.broadcasted_iota(jnp.int32, (BLK, 128), 1)
        line = lax.broadcasted_iota(jnp.int32, (BLK, 128), 0)
        blocks = []
        for s in range(K_NB):
            i = index[pair_column + side, s]
            blocks.append(panels[jnp.where(lax.rem(i // 8, 2) == k, 8 * (i // 16) + lax.rem(i, 8), 64)])
        pick = (lane == line + BLK * side).astype(jnp.bfloat16)
        return lax.dot_general(
            pick, jnp.concatenate(blocks, axis=0), (((1,), (1,)), ((), ())), preferred_element_type=jnp.float32
        ).astype(jnp.bfloat16)

    swaps = []

    def pack():
        own_panel.wait()
        for copy in panel_copies:
            copy.wait_recv()
        halves[0] = pack_side(1 - k)
        swaps.append(remote(halves.at[0], sib_half, half_sem, 0, sibling))
        halves[1] = pack_side(k)

    def add():
        swaps[0].wait_recv()
        packed[pair_column + k] = halves[1] + sib_half[...]

    def row_gather(slot, sems, messages):
        devices = {"P": row_device(1 - zl, y), "R": row_device(zl, ring(y, 1)), "L": row_device(zl, ring(y, -1)),
                   "X": row_device(zl, ring(y, 2))}
        return Gather(slot, y, zl, devices, sems, pending, messages)

    def h_slot(p, w, t):
        return packed.at[p * 4 + w * 2 + k, pl.ds(32 * t, 32)]

    gh = row_gather(h_slot, h_sems, (FORWARD,) * 2)
    h_sib = {}

    def pass_h(i, t):
        slot = h_slot(*gh.need(SLOTS[i], t), t)
        h_sib[i, t] = remote(slot, slot, h_sib_sems, 2 * i + t, sibling)

    def product(source, column):
        stacked = jnp.concatenate([source[index[column, s]] for s in range(K_NB)], axis=0)
        return jnp.dot(packed[column], stacked, preferred_element_type=jnp.float32)

    passes = (0, 1, 2, 3, 5, 4, 6, 7)
    starts = [4 * p + 2 * w for p, w in (gh.at(*SLOTS[i]) for i in passes)]
    across_z = col_device(x, 1 - zh)
    gs = col_gather(ss, s_sems, 2, starts, across_z, S_MESSAGES)

    def first_degree(u):
        if u == 0:
            own_x.wait()
            gx.need_all()
        for t in range(2):
            gh.need(SLOTS[passes[u]], t)
            h_sib[passes[u], t].wait_recv()
        for j in range(2):
            column = starts[u] + j
            at = c * 16 + column
            total = product(xs, column) - center_point * xs[at].astype(jnp.float32)
            ss[at] = (total / half_width).astype(jnp.bfloat16)
        gs.own(u)

    does = {"x": gx.step, "pack": pack, "add": add, "h": gh.step, "p": pass_h, "s": first_degree,
            "g": gs.step}
    for name, *args in FIRST:
        does[name](*args)
    gs.need_all()

    gf = col_gather(fs, f_sems, 4, (0, 4, 8, 12), across_z, F_MESSAGES)

    def r_slot(parity):
        def slot(p, w, t):
            return rows.at[w * 8 + p * 2 + parity, pl.ds(4 * t, 4)]

        return slot

    gr = row_gather(r_slot(k), r_sems, ROW_MESSAGES)
    r_sib = {}

    outs = []

    def write_out(group):
        copy = pltpu.make_async_copy(
            rows.at[group], f_ref.at[:, :, pl.ds(pl.multiple_of(group * 128, 128), 128)], out_sem.at[len(outs)]
        )
        copy.start()
        outs.append(copy)

    def pass_r(i):
        for t in range(4):
            p, w = gr.need(SLOTS[i], t)
        group = w * 8 + p * 2 + k
        r_sib[i] = remote(rows.at[group], rows.at[group], r_sib_sems, i, sibling)
        write_out(group)

    def second_degree(t):
        for j in range(4):
            column = t * 4 + j
            at = c * 16 + column
            total = product(ss, column) - center_point * ss[at].astype(jnp.float32)
            out = ((2.0 / half_width) * total - xs[at].astype(jnp.float32)).astype(jnp.bfloat16)
            fs[at] = out
            rows[r, column] = out
        gf.own(t)
        gr.own(t)

    does = {"f": second_degree, "a": gf.step, "r": gr.step, "q": pass_r}
    for name, *args in SECOND:
        does[name](*args)
    for i in range(8):
        p, w = gr.at(*SLOTS[i])
        r_sib[i].wait_recv()
        write_out(w * 8 + p * 2 + 1 - k)

    def project(which, left):
        def to(place, group):
            for half in range(2):
                place[:, half * 128:(half + 1) * 128] = lax.dot_general(
                    left, rows[group * 2 + half].reshape(1024, 128), (((0,), (0,)), ((), ())),
                    preferred_element_type=jnp.float32,
                ).astype(jnp.bfloat16)

        copies = []
        for i, (xx, z) in enumerate(col_peers):
            group = xx * 2 + z
            to(part.at[which, group], group)
            copies.append(
                remote(part.at[which, group], parts.at[which, c], part_sems, which * 7 + i, col_device(xx, z))
            )
        to(parts.at[which, c], c)
        return copies

    corr_copies = project(0, fs[pl.ds(c * 16, 16)].reshape(1024, 128))
    gf.need_all()

    for column in range(16):
        image[column] = product(fs, column).astype(jnp.bfloat16)

    proj_copies = project(1, image[...].reshape(1024, 128))

    for copy in pending[:-14]:
        copy.wait_send()
    for copy in outs:
        copy.wait()
    for copy in corr_copies:
        copy.wait_recv()
    corr_ref[...] = jnp.sum(parts[0].astype(jnp.float32), axis=0) / 8192.0
    for copy in proj_copies:
        copy.wait_recv()
    proj_ref[...] = jnp.sum(parts[1].astype(jnp.float32), axis=0) / 8192.0
    for copy in corr_copies + proj_copies:
        copy.wait_send()


def shards(hamiltonian, block_cols, start_vectors):
    bf16, f32, dma = jnp.bfloat16, jnp.float32, pltpu.SemaphoreType.DMA
    vmem = pltpu.VMEM
    place = pl.BlockSpec(memory_space=pl.ANY)
    out_shape = (
        jax.ShapeDtypeStruct((16, BLK, 2048), bf16),
        jax.ShapeDtypeStruct((128, 256), f32),
        jax.ShapeDtypeStruct((128, 256), f32),
    )
    results = pl.pallas_call(
        kernel,
        out_shape=out_shape,
        in_specs=[place] * 3,
        out_specs=(place, pl.BlockSpec(memory_space=pltpu.VMEM), pl.BlockSpec(memory_space=pltpu.VMEM)),
        scratch_shapes=[
            vmem((65, BLK, 128), bf16),
            vmem((8, 8, 128), jnp.int32),
            vmem((8, 128), jnp.int32),
            pltpu.SMEM((16, 128), jnp.int32),
            vmem((2, BLK, DEPTH), bf16),
            vmem((BLK, DEPTH), bf16),
            vmem((16, BLK, DEPTH), bf16),
            vmem((128, BLK, 128), bf16),
            vmem((128, BLK, 128), bf16),
            vmem((128, BLK, 128), bf16),
            vmem((16, 16, BLK, 128), bf16),
            vmem((16, BLK, 128), bf16),
            vmem((8, K_NB), jnp.int32),
            vmem((2, 8, 128, 256), bf16),
            vmem((2, 8, 128, 256), bf16),
            dma((3,)),
            dma((2, 7)),
            dma((2, 7)),
            dma((2, 1)),
            dma((2,)),
            dma((2, 1)),
            dma((2, 7, 2)),
            dma((2, 16)),
            dma((2, 7, 2)),
            dma((2, 7, 8)),
            dma((2, 7, 4)),
            dma((2, 7, 4)),
            dma((2, 8)),
            dma((2, 14)),
            dma((16,)),
        ],
        compiler_params=pltpu.CompilerParams(
            collective_id=0, has_side_effects=True, vmem_limit_bytes=48 * 1024 * 1024
        ),
    )(hamiltonian.reshape(8, BLK, 1024), block_cols, start_vectors.reshape(16, BLK, 2048))

    def hand_on(*refs):
        copies = [pltpu.make_async_copy(refs[i], refs[3 + i], refs[6].at[i]) for i in (1, 2)]
        for i in range(4):
            part = pl.ds(4 * i, 4)
            copies.append(pltpu.make_async_copy(refs[0].at[part], refs[3].at[part], refs[6].at[3 + i]))
        for copy in copies:
            copy.start()
        for copy in copies:
            copy.wait()

    f, corr, proj = pl.pallas_call(
        hand_on,
        out_shape=out_shape,
        in_specs=[place] * 3,
        out_specs=(place,) * 3,
        scratch_shapes=[dma((7,))],
        compiler_params=pltpu.CompilerParams(vmem_limit_bytes=40 * 1024 * 1024),
    )(*results)
    return f.reshape(1024, 2048), corr, proj


def solution(mesh):
    in_specs = (P("row", "col"), P("row", None), P("col", None))
    out_specs = (P("col", None), P("row", "col"), P("row", "col"))
    return jax.shard_map(shards, mesh=mesh, in_specs=in_specs, out_specs=out_specs, check_vma=False)
```
